32 devices in a mesh: grp: 4 (over x, core), rep: 8 (over z, y).
Axes of the slice: x: 2, y: 2, z: 4, core: 2. Of those that a mesh axis runs over, the one named last changes fastest.
Arguments:
- blocks: bfloat16 [64, 64, 4096], P(('grp', 'rep')), may hold values from 0 to 10
- coords: int32 [64, 3], P(('grp', 'rep')), may hold values from 0 to 63, as said below
- factor_a: float32 [2048, 128], P(('grp', 'rep')), may hold values from 0 to 1
- factor_b: bfloat16 [4096, 128], P('grp'), may hold values from 0.049804688 to 1
- factor_c: bfloat16 [4096, 128], P('grp'), may hold values from 0.049804688 to 1
Outputs:
- updated_a: float32 [2048, 128], P(('grp', 'rep'))
The draws below stay inside these ranges and needn't reach their ends.
Inputs may be any that keep to these rules, and one draw needn't show every extreme that they name: Row n of coords holds first, second and third coordinates below 32, 64, 64. Among the 2 blocks of one device, for each mode, the values coordinate // 8 (first mode) or coordinate // 16 (second and third) take any one value at most 2 times.
All inputs are finite; a program needn't handle non-finite values.
Results may differ from the reference program's by a relative error of at most 0.00072.
Values may be sent and summed in bfloat16 or wider, within the bound.
No kernel may reach another device: no remote copies, remote signals or barrier semaphores. Data moves between devices by JAX's collectives and lax.ppermute only.
A program may use at most 64 MiB of HBM per device.

```python
import math
import jax
import jax.numpy as jnp
from jax import lax

R = 128
BS = 64
NBLK = 2
JB_DEV = 16
CAP = 2
PART_BLK = 8
IBLK = 32
JBLK = 64
N_GRP = 4
DEVICES = 32


def draw_coords(key, part):

    def per_device(device):
        dev_key = jax.random.fold_in(key, device)
        columns = []
        for mode_idx, extent in ((0, PART_BLK), (1, JB_DEV), (2, JB_DEV)):
            order_pos = jax.random.permutation(jax.random.fold_in(dev_key, 3 * mode_idx), NBLK)
            owners_perm = jax.random.permutation(jax.random.fold_in(dev_key, 3 * mode_idx + 1), N_GRP)
            owner = owners_perm[order_pos // CAP]
            offset = jax.random.randint(jax.random.fold_in(dev_key, 3 * mode_idx + 2), (NBLK,), 0, extent)
            columns.append(owner * extent + offset)
        return jnp.stack(columns, 1)
    return jax.vmap(per_device)(jnp.arange(DEVICES)).reshape(-1, 3).astype(jnp.int32)


def block_levels(key, shape, cuts, least, largest):
    def one(position, blocks):
        draws = jax.random.uniform(jax.random.fold_in(jax.random.fold_in(key, 6), position), (blocks,), jnp.float32, least / len(cuts), largest / len(cuts))
        return jnp.repeat(jnp.exp(draws), shape[position] // blocks).reshape((-1,) + (1,) * (len(shape) - position - 1))

    factor_of = one(*cuts[0])
    for cut in cuts[1:]:
        factor_of = factor_of * one(*cut)
    return factor_of


def setup_inputs(seed: int = 0) -> dict:
    splits = jax.random.split(jax.random.key(seed), 6)
    blocks = jnp.clip(10.0 * jax.random.uniform(splits[0], (DEVICES * NBLK, BS, BS * BS), jnp.float32) ** block_levels(splits[0], (DEVICES * NBLK, BS, BS * BS), ((0, 32),), -0.2, 0.2), 0.0, 10.0).astype(jnp.bfloat16)
    coords = draw_coords(jax.random.fold_in(splits[5], 71), 0)
    factor_a = jnp.clip(1.0 * jax.random.uniform(splits[2], (IBLK * BS, R), jnp.float32) ** block_levels(splits[2], (IBLK * BS, R), ((0, 32),), -0.2, 0.2), 0.0, 1.0)
    factor_b = jnp.clip(jnp.exp(math.log(1.0) - 2.9996462 * jax.random.uniform(splits[3], (JBLK * BS, R), jnp.float32) ** block_levels(splits[3], (JBLK * BS, R), ((0, 4),), -0.2, 0.2)), 0.049804688, 1.0).astype(jnp.bfloat16)
    factor_c = jnp.clip(jnp.exp(math.log(1.0) - 2.9996462 * jax.random.uniform(splits[4], (JBLK * BS, R), jnp.float32) ** block_levels(splits[4], (JBLK * BS, R), ((0, 4),), -0.2, 0.2)), 0.049804688, 1.0).astype(jnp.bfloat16)
    return dict(blocks=blocks, coords=coords, factor_a=factor_a, factor_b=factor_b, factor_c=factor_c)


def reference(blocks, coords, factor_a, factor_b, factor_c):
    rows_b = factor_b.reshape(-1, BS, R)
    rows_c = factor_c.reshape(-1, BS, R)

    def per_block(pair):
        block_x, coord_row = pair
        left = rows_b[coord_row[1]].astype(jnp.float32)
        right = rows_c[coord_row[2]].astype(jnp.float32)
        khatri = (left[:, None, :] * right[None, :, :]).astype(jnp.bfloat16).reshape(BS * BS, R)
        return jnp.dot(block_x, khatri, preferred_element_type=jnp.float32)
    partial_rows = lax.map(per_block, (blocks, coords))
    mttkrp = jnp.zeros((IBLK, BS, R), jnp.float32).at[coords[:, 0]].add(partial_rows).reshape(IBLK * BS, R)
    dims = (((0,), (0,)), ((), ()))
    gram_b = lax.dot_general(factor_b, factor_b, dims, preferred_element_type=jnp.float32)
    gram_c = lax.dot_general(factor_c, factor_c, dims, preferred_element_type=jnp.float32)
    norm_b = jnp.sqrt(jnp.diagonal(gram_b))
    norm_c = jnp.sqrt(jnp.diagonal(gram_c))
    gram = gram_b / (norm_b[:, None] * norm_b[None, :]) * (gram_c / (norm_c[:, None] * norm_c[None, :]))
    target = mttkrp / (norm_b * norm_c)[None, :]

    def column_step(column, factor):
        g_column = lax.dynamic_slice_in_dim(gram, column, 1, 1)
        predicted = jnp.dot(factor, g_column, precision=lax.Precision.HIGHEST)
        m_column = lax.dynamic_slice_in_dim(target, column, 1, 1)
        a_column = lax.dynamic_slice_in_dim(factor, column, 1, 1)
        pivot = lax.dynamic_slice_in_dim(g_column, column, 1, 0)
        updated = jnp.maximum(a_column + (m_column - predicted) / pivot, 0.0)
        return lax.dynamic_update_slice_in_dim(factor, updated, column, 1)
    return lax.fori_loop(0, R, column_step, factor_a)
```

```python
import functools

import jax
import jax.numpy as jnp
from jax import lax
from jax.experimental import pallas as pl
from jax.experimental.pallas import tpu as pltpu
from jax.sharding import PartitionSpec as P

BS = 64
TILE = 8
CORES = 2
EXACT = lax.Precision.HIGHEST
VMEM = pl.BlockSpec(memory_space=pltpu.VMEM)
SMEM = pl.BlockSpec(memory_space=pltpu.SMEM)
ANY = pl.BlockSpec(memory_space=pl.ANY)


def shift_grp(value, n_grp, chips, swap):
    n_x = n_grp // CORES
    pairs = [
        (x * CORES + c, ((x + chips) % n_x) * CORES + (c ^ swap))
        for x in range(n_x)
        for c in range(CORES)
    ]
    return lax.ppermute(value, "grp", pairs)


def gather_kernel(n_ask, nblk, jb, here_ref, *refs):
    asks, (own_b, own_c, mate_b, mate_c) = refs[:n_ask], refs[n_ask : n_ask + 4]
    outs, sems = refs[n_ask + 4 : -1], refs[-1]
    core = lax.rem(here_ref[0], CORES)
    copies = []
    for a in range(n_ask):
        for mode, (own, mate) in enumerate(((own_b, mate_b), (own_c, mate_c))):
            for n in range(nblk):
                slot = mode * nblk + n
                local = lax.rem(asks[a][n, 1 + mode], CORES * jb)
                row = pl.multiple_of(lax.rem(local, jb) * BS, BS)
                is_own = lax.div(local, jb) == core
                dst, sem = outs[a].at[slot], sems.at[a * 2 * nblk + slot]
                from_own = pltpu.make_async_copy(own.at[pl.ds(row, BS)], dst, sem)
                from_mate = pltpu.make_async_copy(mate.at[pl.ds(row, BS)], dst, sem)
                pl.when(is_own)(from_own.start)
                pl.when(jnp.logical_not(is_own))(from_mate.start)
                copies.append(from_own)
    for copy in copies:
        copy.wait()


def gram_kernel(own_b, mate_b, own_c, mate_c, out_ref):
    dims = (((0,), (0,)), ((), ()))
    for mode, pair in enumerate(((own_b, mate_b), (own_c, mate_c))):
        total = 0.0
        for ref in pair:
            total += lax.dot_general(ref[...], ref[...], dims, preferred_element_type=jnp.float32)
        out_ref[mode] = total


def partial_kernel(n_x, nblk, jb, here_ref, ask_ref, *refs):
    found, blocks_ref, out_ref = refs[:n_x], refs[n_x], refs[n_x + 1]
    my_x = lax.div(here_ref[0], CORES)

    def rows_of(n, mode):
        chip = lax.div(ask_ref[n, 1 + mode], CORES * jb)
        slot = mode * nblk + n
        rows = found[0][slot]
        for d in range(1, n_x):
            rows = jnp.where(chip == lax.rem(my_x + d, n_x), found[d][slot], rows)
        return rows.astype(jnp.float32)

    step = 8
    for n in range(nblk):
        left, right = rows_of(n, 0), rows_of(n, 1)
        rank = left.shape[1]
        total = jnp.zeros((BS, rank), jnp.float32)
        for j in range(0, BS, step):
            khatri = (left[j : j + step, None, :] * right[None, :, :]).astype(jnp.bfloat16)
            total += jnp.dot(
                blocks_ref[n, :, j * BS : (j + step) * BS],
                khatri.reshape(step * BS, rank),
                preferred_element_type=jnp.float32,
            )
        out_ref[n, :BS] = total
        out_ref[n, BS:] = jnp.full((TILE, rank), ask_ref[n, 0].astype(jnp.float32))


def dispatch_kernel(nblk, n_rep, ab, here_ref, *refs):
    arrived, out_ref = refs[:-1], refs[-1]
    first = here_ref[0] * (n_rep * ab)

    def fill(owner, sub):
        target = (first + owner * ab + sub).astype(jnp.float32)
        total = None
        for ref in arrived:
            for n in range(nblk):
                term = jnp.where(ref[n, BS : BS + 1] == target, ref[n, :BS], 0.0)
                total = term if total is None else total + term
        out_ref[owner, sub * BS : (sub + 1) * BS] = total

    for sub in range(ab):
        if n_rep <= 8:
            for owner in range(n_rep):
                fill(owner, sub)
        else:
            pl.loop(0, n_rep)(functools.partial(fill, sub=sub))


def prepare_kernel(n_x, *refs):
    grams, a_ref, low_ref, pre_ref, scale_ref = refs[:n_x], *refs[n_x:]
    gram_b, gram_c = grams[0][0], grams[0][1]
    for ref in grams[1:]:
        gram_b += ref[0]
        gram_c += ref[1]
    shape = gram_b.shape
    at_row = lax.broadcasted_iota(jnp.int32, shape, 0)
    at_col = lax.broadcasted_iota(jnp.int32, shape, 1)

    def diagonal(square, axis):
        return jnp.sum(jnp.where(at_row == at_col, square, 0.0), axis=axis, keepdims=True)

    norm_b_row, norm_b_col = jnp.sqrt(diagonal(gram_b, 0)), jnp.sqrt(diagonal(gram_b, 1))
    norm_c_row, norm_c_col = jnp.sqrt(diagonal(gram_c, 0)), jnp.sqrt(diagonal(gram_c, 1))
    gram = gram_b / (norm_b_col * norm_b_row) * (gram_c / (norm_c_col * norm_c_row))
    pivot = diagonal(gram, 1)
    steps = gram.T / pivot
    low_ref[...] = jnp.where(at_col < at_row, steps, 0.0)
    later = jnp.where(at_col > at_row, steps, 0.0)
    pre_ref[...] = lax.dot_general(
        later, a_ref[...], (((1,), (1,)), ((), ())), precision=EXACT, preferred_element_type=jnp.float32
    )
    scale_ref[...] = jnp.broadcast_to(1.0 / (norm_b_col * norm_c_col * pivot), scale_ref.shape)


def sweep_kernel(n_rep, low_ref, pre_ref, scale_ref, sums_ref, out_ref):
    rank, rows = pre_ref.shape
    if n_rep <= 8:
        total = sums_ref[0]
        for i in range(1, n_rep):
            total += sums_ref[i]
    else:
        total = lax.fori_loop(1, n_rep, lambda i, acc: acc + sums_ref[i], sums_ref[0])
    start = total.T * scale_ref[...] - pre_ref[...]
    count = rank // TILE
    rest = [start[t * TILE : (t + 1) * TILE] for t in range(count)]
    for k in range(count):
        for s in range(TILE):
            column = k * TILE + s
            done = jnp.broadcast_to(jnp.maximum(rest[k], 0.0)[s : s + 1], (TILE, rows))
            for t in range(k if s < TILE - 1 else k + 1, count):
                weight = low_ref[t * TILE : (t + 1) * TILE, column : column + 1]
                rest[t] = rest[t] - weight * done
        rest[k] = jnp.maximum(rest[k], 0.0)
    out_ref[...] = jnp.concatenate(rest, 0).T


def body(blocks, coords, factor_a, factor_b, factor_c):
    n_grp = lax.axis_size("grp")
    n_rep = lax.axis_size("rep")
    n_x = n_grp // CORES
    nblk = blocks.shape[0]
    rank = factor_a.shape[1]
    jb = factor_b.shape[0] // BS
    ab = factor_a.shape[0] // BS
    here = lax.axis_index("grp").astype(jnp.int32).reshape(1)

    asks = [coords] + [shift_grp(coords, n_grp, d, 0) for d in range(1, n_x)]
    mate_b = shift_grp(factor_b, n_grp, 0, 1)
    mate_c = shift_grp(factor_c, n_grp, 0, 1)

    rows_shape = jax.ShapeDtypeStruct((2 * nblk, BS, rank), factor_b.dtype)
    answers = pl.pallas_call(
        functools.partial(gather_kernel, n_x, nblk, jb),
        out_shape=[rows_shape] * n_x,
        in_specs=[SMEM] * (1 + n_x) + [ANY] * 4,
        out_specs=[VMEM] * n_x,
        scratch_shapes=[pltpu.SemaphoreType.DMA((n_x * 2 * nblk,))],
        name="gather_rows",
    )(here, *asks, factor_b, factor_c, mate_b, mate_c)
    found = [answers[0]] + [shift_grp(answers[d], n_grp, -d, 0) for d in range(1, n_x)]

    chip_gram = pl.pallas_call(
        gram_kernel,
        out_shape=jax.ShapeDtypeStruct((2, rank, rank), jnp.float32),
        in_specs=[VMEM] * 4,
        out_specs=VMEM,
        name="chip_gram",
    )(factor_b, mate_b, factor_c, mate_c)
    grams = [chip_gram] + [shift_grp(chip_gram, n_grp, d, 0) for d in range(1, n_x)]

    partial = pl.pallas_call(
        functools.partial(partial_kernel, n_x, nblk, jb),
        out_shape=jax.ShapeDtypeStruct((nblk, BS + TILE, rank), jnp.float32),
        in_specs=[SMEM] * 2 + [VMEM] * (n_x + 1),
        out_specs=VMEM,
        name="block_products",
    )(here, coords, *found, blocks)
    arrived = [
        shift_grp(partial, n_grp, d, swap) if d or swap else partial
        for d in range(n_x)
        for swap in range(CORES)
    ]

    dense = pl.pallas_call(
        functools.partial(dispatch_kernel, nblk, n_rep, ab),
        out_shape=jax.ShapeDtypeStruct((n_rep, ab * BS, rank), jnp.float32),
        in_specs=[SMEM] + [VMEM] * n_grp,
        out_specs=VMEM,
        name="sum_by_owner",
    )(here, *arrived)
    sums = lax.all_to_all(dense, "rep", split_axis=0, concat_axis=0, tiled=True)

    low, pre, scale = pl.pallas_call(
        functools.partial(prepare_kernel, n_x),
        out_shape=[
            jax.ShapeDtypeStruct((rank, rank), jnp.float32),
            jax.ShapeDtypeStruct((rank, ab * BS), jnp.float32),
            jax.ShapeDtypeStruct((rank, ab * BS), jnp.float32),
        ],
        in_specs=[VMEM] * (n_x + 1),
        out_specs=[VMEM] * 3,
        name="prepare_sweep",
    )(*grams, factor_a)
    return pl.pallas_call(
        functools.partial(sweep_kernel, n_rep),
        out_shape=jax.ShapeDtypeStruct(factor_a.shape, jnp.float32),
        in_specs=[VMEM] * 4,
        out_specs=VMEM,
        name="sweep",
    )(low, pre, scale, sums)


def solution(mesh):
    placed = (
        P(("grp", "rep"), None, None),
        P(("grp", "rep"), None),
        P(("grp", "rep"), None),
        P("grp", None),
        P("grp", None),
    )
    return jax.shard_map(
        body, mesh=mesh, in_specs=placed, out_specs=P(("grp", "rep"), None), check_vma=False
    )
```

```python
import functools

import jax
import jax.numpy as jnp
from jax import lax
from jax.experimental import pallas as pl
from jax.experimental.pallas import tpu as pltpu
from jax.sharding import PartitionSpec as P

BS = 64
TILE = 8
CORES = 2
EXACT = lax.Precision.HIGHEST
VMEM = pl.BlockSpec(memory_space=pltpu.VMEM)
HBM = pl.BlockSpec(memory_space=pltpu.HBM)
SMEM = pl.BlockSpec(memory_space=pltpu.SMEM)


def moves(n_grp, n_rep, to):
    pairs = []
    for g in range(n_grp):
        for rep in range(n_rep):
            x, c, to_rep = to(g // CORES, g % CORES, rep)
            pairs.append((g * n_rep + rep, (x * CORES + c) * n_rep + to_rep))
    return pairs


def partner(index, offset, size):
    return index ^ offset if size & (size - 1) == 0 else (index + offset) % size


def here():
    grp = lax.axis_index("grp")
    return lax.div(grp, CORES), lax.rem(grp, CORES), lax.axis_index("rep")


def load_kernel(b_ref, c_ref, own_b, own_c, sems):
    copies = [
        pltpu.make_async_copy(src, dst, sems.at[i])
        for i, (src, dst) in enumerate(((b_ref, own_b), (c_ref, own_c)))
    ]
    for copy in copies:
        copy.start()
    for copy in copies:
        copy.wait()


def gram_kernel(own_b, mate_b, own_c, mate_c, out_ref):
    _, core, _ = here()
    dims = (((0,), (0,)), ((), ()))

    def fill(*shards):
        total = 0.0
        for ref in shards:
            total += lax.dot_general(ref[...], ref[...], dims, preferred_element_type=jnp.float32)
        out_ref[...] = total

    pl.when(core == 0)(lambda: fill(own_b, mate_b))
    pl.when(core != 0)(lambda: fill(own_c, mate_c))


def row_block(own, mate, local, core, jb):
    row = pl.multiple_of(lax.rem(local, jb) * BS, BS)
    return jnp.where(lax.div(local, jb) == core, own[pl.ds(row, BS)], mate[pl.ds(row, BS)])


def gather_kernel(n_ask, nblk, jb, *refs):
    asks, factors, outs = refs[:n_ask], refs[n_ask : n_ask + 4], refs[n_ask + 4 :]
    _, core, _ = here()
    for ask, out in zip(asks, outs):
        for mode in range(2):
            for n in range(nblk):
                local = lax.rem(ask[n, 1 + mode], CORES * jb)
                out[mode * nblk + n] = row_block(*factors[2 * mode : 2 * mode + 2], local, core, jb)


def local_kernel(n_x, nblk, jb, ask_ref, *refs):
    factors, (rows_ref, far_ref, first_ref) = refs[:4], refs[4:]
    my_x, core, _ = here()
    for mode in range(2):
        for n in range(nblk):
            slot = mode * nblk + n
            wanted = ask_ref[n, 1 + mode]
            local = lax.rem(wanted, CORES * jb)
            rows_ref[slot] = row_block(*factors[2 * mode : 2 * mode + 2], local, core, jb)
            far = lax.rem(lax.div(wanted, CORES * jb) - my_x + n_x, n_x)
            far_ref[slot] = jnp.full(far_ref.shape[1:], far, jnp.int32)
    for n in range(nblk):
        first_ref[n] = jnp.full(first_ref.shape[1:], ask_ref[n, 0].astype(jnp.float32))


def partial_kernel(n_x, nblk, rows_ref, far_ref, first_ref, *refs):
    found, blocks_ref, out_ref = refs[:-2], refs[-2], refs[-1]

    def rows_of(n, mode):
        slot = mode * nblk + n
        rows = rows_ref[slot].astype(jnp.float32)
        for d in range(1, n_x):
            rows = jnp.where(far_ref[slot, :1] == d, found[d - 1][slot].astype(jnp.float32), rows)
        return rows

    step = 8
    for n in range(nblk):
        left, right = rows_of(n, 0), rows_of(n, 1)
        rank = left.shape[1]
        total = jnp.zeros((BS, rank), jnp.float32)
        for j in range(0, BS, step):
            khatri = (left[j : j + step, None, :] * right[None, :, :]).astype(jnp.bfloat16)
            total += jnp.dot(
                blocks_ref[n, :, j * BS : (j + step) * BS],
                khatri.reshape(step * BS, rank),
                preferred_element_type=jnp.float32,
            )
        out_ref[n, :BS] = total
        out_ref[n, BS:] = first_ref[n]


def owner_kernel(n_rep, near, ab, count, *refs):
    arrived, outs = refs[:count], refs[count:]
    my_x, core, rep = here()
    line = n_rep // near
    at, side = lax.div(rep, near), lax.rem(rep, near)
    for offset, out in enumerate(outs):
        if line & (line - 1) == 0:
            to_at = lax.bitwise_xor(at, offset)
        else:
            to_at = lax.rem(at + offset, line)
        to_core = core if offset == 0 else 1 - core
        first = ((my_x * CORES + to_core) * n_rep + to_at * near + side) * ab
        for sub in range(ab):
            target = (first + sub).astype(jnp.float32)
            total = None
            for ref in arrived:
                for n in range(ref.shape[0]):
                    term = jnp.where(ref[n, BS : BS + 1] == target, ref[n, :BS], 0.0)
                    total = term if total is None else total + term
            out[sub * BS : (sub + 1) * BS] = total


def prepare_kernel(gram_b_ref, gram_c_ref, a_ref, low_ref, pre_ref, scale_ref):
    gram_b, gram_c = gram_b_ref[...], gram_c_ref[...]
    shape = gram_b.shape
    at_row = lax.broadcasted_iota(jnp.int32, shape, 0)
    at_col = lax.broadcasted_iota(jnp.int32, shape, 1)

    def diagonal(square, axis):
        return jnp.sum(jnp.where(at_row == at_col, square, 0.0), axis=axis, keepdims=True)

    norm_b_row, norm_b_col = jnp.sqrt(diagonal(gram_b, 0)), jnp.sqrt(diagonal(gram_b, 1))
    norm_c_row, norm_c_col = jnp.sqrt(diagonal(gram_c, 0)), jnp.sqrt(diagonal(gram_c, 1))
    gram = gram_b / (norm_b_col * norm_b_row) * (gram_c / (norm_c_col * norm_c_row))
    pivot = diagonal(gram, 1)
    steps = gram.T / pivot
    low_ref[...] = jnp.where(at_col < at_row, steps, 0.0)
    later = jnp.where(at_col > at_row, steps, 0.0)
    pre_ref[...] = lax.dot_general(
        later, a_ref[...], (((1,), (1,)), ((), ())), precision=EXACT, preferred_element_type=jnp.float32
    )
    scale_ref[...] = jnp.broadcast_to(1.0 / (norm_b_col * norm_c_col * pivot), scale_ref.shape)


def sweep_kernel(low_ref, pre_ref, scale_ref, *refs):
    sums, out_ref = refs[:-1], refs[-1]
    rank, rows = pre_ref.shape
    total = sums[0][...]
    for ref in sums[1:]:
        total += ref[...]
    start = total.T * scale_ref[...] - pre_ref[...]
    count = rank // TILE
    rest = [start[t * TILE : (t + 1) * TILE] for t in range(count)]
    for k in range(count):
        for s in range(TILE):
            column = k * TILE + s
            done = jnp.broadcast_to(jnp.maximum(rest[k], 0.0)[s : s + 1], (TILE, rows))
            for t in range(k if s < TILE - 1 else k + 1, count):
                weight = low_ref[t * TILE : (t + 1) * TILE, column : column + 1]
                rest[t] = rest[t] - weight * done
        rest[k] = jnp.maximum(rest[k], 0.0)
    out_ref[...] = jnp.concatenate(rest, 0).T


def body(blocks, coords, factor_a, factor_b, factor_c):
    n_grp = lax.axis_size("grp")
    n_rep = lax.axis_size("rep")
    n_x = n_grp // CORES
    near = 2 if n_rep % 2 == 0 else 1
    line = n_rep // near
    nblk = blocks.shape[0]
    rank = factor_a.shape[1]
    jb = factor_b.shape[0] // BS
    ab = factor_a.shape[0] // BS
    params = pltpu.CompilerParams(vmem_limit_bytes=16 * 2**20)

    def move(value, chips, swap, beside=0, along=0):
        def to(x, c, rep):
            to_rep = partner(rep // near, along, line) * near + ((rep + beside) % near)
            return (x + chips) % n_x, c ^ swap, to_rep

        return lax.ppermute(value, ("grp", "rep"), moves(n_grp, n_rep, to))

    asks = [move(coords, d, 1) for d in range(1, n_x)]
    mate_b = move(factor_b, 0, 1)
    mate_c = move(factor_c, 0, 1)
    own_b, own_c = pl.pallas_call(
        load_kernel,
        out_shape=[jax.ShapeDtypeStruct(factor_b.shape, factor_b.dtype)] * 2,
        in_specs=[HBM] * 2,
        out_specs=[VMEM] * 2,
        scratch_shapes=[pltpu.SemaphoreType.DMA((2,))],
        compiler_params=params,
        name="load_shards",
    )(factor_b, factor_c)
    factors = (own_b, mate_b, own_c, mate_c)

    chip_gram = pl.pallas_call(
        gram_kernel,
        out_shape=jax.ShapeDtypeStruct((rank, rank), jnp.float32),
        in_specs=[VMEM] * 4,
        out_specs=VMEM,
        compiler_params=params,
        name="chip_gram",
    )(*factors)
    asks, chip_gram = lax.optimization_barrier((asks, chip_gram))

    answers = pl.pallas_call(
        functools.partial(gather_kernel, n_x - 1, nblk, jb),
        out_shape=[jax.ShapeDtypeStruct((2 * nblk, BS, rank), factor_b.dtype)] * (n_x - 1),
        in_specs=[SMEM] * (n_x - 1) + [VMEM] * 4,
        out_specs=[VMEM] * (n_x - 1),
        compiler_params=params,
        name="gather_rows",
    )(*asks, *factors)
    answers, chip_gram = lax.optimization_barrier((answers, chip_gram))
    found = [move(answers[d - 1], -d, 1) for d in range(1, n_x)]
    gram = chip_gram
    for d in range(1, n_x):
        gram = gram + move(chip_gram, d, 0)

    local = pl.pallas_call(
        functools.partial(local_kernel, n_x, nblk, jb),
        out_shape=[
            jax.ShapeDtypeStruct((2 * nblk, BS, rank), factor_b.dtype),
            jax.ShapeDtypeStruct((2 * nblk, TILE, rank), jnp.int32),
            jax.ShapeDtypeStruct((nblk, TILE, rank), jnp.float32),
        ],
        in_specs=[SMEM] + [VMEM] * 4,
        out_specs=[VMEM] * 3,
        compiler_params=params,
        name="local_rows",
    )(coords, *factors)
    found, local = lax.optimization_barrier((found, local))

    partial = pl.pallas_call(
        functools.partial(partial_kernel, n_x, nblk),
        out_shape=jax.ShapeDtypeStruct((nblk, BS + TILE, rank), jnp.float32),
        in_specs=[VMEM] * (3 + n_x),
        out_specs=VMEM,
        compiler_params=params,
        name="block_products",
    )(*local, *found, blocks)
    others = [
        move(partial, d, 1, beside)
        for d in range(n_x)
        for beside in range(near)
        if d or beside
    ]
    prepared = pl.pallas_call(
        prepare_kernel,
        out_shape=[
            jax.ShapeDtypeStruct((rank, rank), jnp.float32),
            jax.ShapeDtypeStruct((rank, ab * BS), jnp.float32),
            jax.ShapeDtypeStruct((rank, ab * BS), jnp.float32),
        ],
        in_specs=[VMEM] * 3,
        out_specs=[VMEM] * 3,
        compiler_params=params,
        name="prepare_sweep",
    )(gram, move(gram, 0, 1), factor_a)
    arrived = [partial, move(partial, 0, 1), *others, *(move(value, 0, 1) for value in others)]

    sums = pl.pallas_call(
        functools.partial(owner_kernel, n_rep, near, ab, len(arrived)),
        out_shape=[jax.ShapeDtypeStruct(factor_a.shape, jnp.float32)] * line,
        in_specs=[VMEM] * len(arrived),
        out_specs=[VMEM] * line,
        compiler_params=params,
        name="sum_by_owner",
    )(*arrived)
    sums = [sums[0]] + [move(sums[d], 0, 1, 0, d) for d in range(1, line)]

    return pl.pallas_call(
        sweep_kernel,
        out_shape=jax.ShapeDtypeStruct(factor_a.shape, jnp.float32),
        in_specs=[VMEM] * (3 + line),
        out_specs=VMEM,
        compiler_params=params,
        name="sweep",
    )(*prepared, *sums)


def solution(mesh):
    placed = (
        P(("grp", "rep"), None, None),
        P(("grp", "rep"), None),
        P(("grp", "rep"), None),
        P("grp", None),
        P("grp", None),
    )
    return jax.shard_map(
        body, mesh=mesh, in_specs=placed, out_specs=P(("grp", "rep"), None), check_vma=False
    )
```

```python
import functools

import jax
import jax.numpy as jnp
from jax import lax
from jax.experimental import pallas as pl
from jax.experimental.pallas import tpu as pltpu
from jax.sharding import PartitionSpec as P

BS = 64
TILE = 8
CORES = 2
EXACT = lax.Precision.HIGHEST
VMEM = pl.BlockSpec(memory_space=pltpu.VMEM)
HBM = pl.BlockSpec(memory_space=pltpu.HBM)
SMEM = pl.BlockSpec(memory_space=pltpu.SMEM)


def moves(n_grp, n_rep, to):
    pairs = []
    for g in range(n_grp):
        for rep in range(n_rep):
            x, c, to_rep = to(g // CORES, g % CORES, rep)
            pairs.append((g * n_rep + rep, (x * CORES + c) * n_rep + to_rep))
    return pairs


def partner(index, offset, size):
    return index ^ offset if size & (size - 1) == 0 else (index + offset) % size


def here():
    grp = lax.axis_index("grp")
    return lax.div(grp, CORES), lax.rem(grp, CORES), lax.axis_index("rep")


def load_kernel(b_ref, c_ref, own_b, own_c, sems):
    copies = [
        pltpu.make_async_copy(src, dst, sems.at[i])
        for i, (src, dst) in enumerate(((b_ref, own_b), (c_ref, own_c)))
    ]
    for copy in copies:
        copy.start()
    for copy in copies:
        copy.wait()


def gram_kernel(own_b, mate_b, own_c, mate_c, out_ref):
    _, core, _ = here()
    dims = (((0,), (0,)), ((), ()))

    def fill(*shards):
        total = 0.0
        for ref in shards:
            total += lax.dot_general(ref[...], ref[...], dims, preferred_element_type=jnp.float32)
        out_ref[...] = total

    pl.when(core == 0)(lambda: fill(own_b, mate_b))
    pl.when(core != 0)(lambda: fill(own_c, mate_c))


def row_block(own, mate, local, core, jb):
    row = pl.multiple_of(lax.rem(local, jb) * BS, BS)
    return jnp.where(lax.div(local, jb) == core, own[pl.ds(row, BS)], mate[pl.ds(row, BS)])


def gather_kernel(n_ask, nblk, jb, *refs):
    asks, factors, outs = refs[:n_ask], refs[n_ask : n_ask + 4], refs[n_ask + 4 :]
    _, core, _ = here()
    for ask, out in zip(asks, outs):
        for mode in range(2):
            for n in range(nblk):
                local = lax.rem(ask[n, 1 + mode], CORES * jb)
                out[mode * nblk + n] = row_block(*factors[2 * mode : 2 * mode + 2], local, core, jb)


def local_kernel(n_x, nblk, jb, ask_ref, *refs):
    factors, (rows_ref, far_ref, first_ref) = refs[:4], refs[4:]
    my_x, core, _ = here()
    for mode in range(2):
        for n in range(nblk):
            slot = mode * nblk + n
            wanted = ask_ref[n, 1 + mode]
            local = lax.rem(wanted, CORES * jb)
            rows_ref[slot] = row_block(*factors[2 * mode : 2 * mode + 2], local, core, jb)
            far = lax.rem(lax.div(wanted, CORES * jb) - my_x + n_x, n_x)
            far_ref[slot] = jnp.full(far_ref.shape[1:], far, jnp.int32)
    for n in range(nblk):
        first_ref[n] = jnp.full(first_ref.shape[1:], ask_ref[n, 0].astype(jnp.float32))


def partial_kernel(n_x, nblk, rows_ref, far_ref, first_ref, *refs):
    found, blocks_ref, out_ref = refs[:-2], refs[-2], refs[-1]

    def rows_of(n, mode):
        slot = mode * nblk + n
        rows = rows_ref[slot].astype(jnp.float32)
        for d in range(1, n_x):
            rows = jnp.where(far_ref[slot, :1] == d, found[d - 1][slot].astype(jnp.float32), rows)
        return rows

    step = 8
    for n in range(nblk):
        left, right = rows_of(n, 0), rows_of(n, 1)
        rank = left.shape[1]
        total = jnp.zeros((BS, rank), jnp.float32)
        for j in range(0, BS, step):
            khatri = (left[j : j + step, None, :] * right[None, :, :]).astype(jnp.bfloat16)
            total += jnp.dot(
                blocks_ref[n, :, j * BS : (j + step) * BS],
                khatri.reshape(step * BS, rank),
                preferred_element_type=jnp.float32,
            )
        out_ref[n, :BS] = total
        out_ref[n, BS:] = first_ref[n]


def owner_kernel(n_rep, near, ab, count, *refs):
    arrived, outs = refs[:count], refs[count:]
    my_x, core, rep = here()
    line = n_rep // near
    at, side = lax.div(rep, near), lax.rem(rep, near)
    for offset, out in enumerate(outs):
        if line & (line - 1) == 0:
            to_at = lax.bitwise_xor(at, offset)
        else:
            to_at = lax.rem(at + offset, line)
        to_core = core if offset == 0 else 1 - core
        first = ((my_x * CORES + to_core) * n_rep + to_at * near + side) * ab
        for sub in range(ab):
            target = (first + sub).astype(jnp.float32)
            total = None
            for ref in arrived:
                for n in range(ref.shape[0]):
                    term = jnp.where(ref[n, BS : BS + 1] == target, ref[n, :BS], 0.0)
                    total = term if total is None else total + term
            out[sub * BS : (sub + 1) * BS] = total


def prepare_kernel(gram_b_ref, gram_c_ref, a_ref, within_ref, after_ref, pre_ref, scale_ref, low_ref):
    gram_b, gram_c = gram_b_ref[...], gram_c_ref[...]
    shape = gram_b.shape
    at_row = lax.broadcasted_iota(jnp.int32, shape, 0)
    at_col = lax.broadcasted_iota(jnp.int32, shape, 1)

    def diagonal(square, axis):
        return jnp.sum(jnp.where(at_row == at_col, square, 0.0), axis=axis, keepdims=True)

    norm_b_row, norm_b_col = jnp.sqrt(diagonal(gram_b, 0)), jnp.sqrt(diagonal(gram_b, 1))
    norm_c_row, norm_c_col = jnp.sqrt(diagonal(gram_c, 0)), jnp.sqrt(diagonal(gram_c, 1))
    gram = gram_b / (norm_b_col * norm_b_row) * (gram_c / (norm_c_col * norm_c_row))
    pivot = diagonal(gram, 1)
    steps = gram.T / pivot
    low_ref[...] = jnp.where(at_col < at_row, steps, 0.0)
    later = jnp.where(at_col > at_row, steps, 0.0)
    pre_ref[...] = lax.dot_general(
        later, a_ref[...], (((1,), (1,)), ((), ())), precision=EXACT, preferred_element_type=jnp.float32
    )
    scale_ref[...] = jnp.broadcast_to(1.0 / (norm_b_col * norm_c_col * pivot), scale_ref.shape)
    count, tile = shape[0] // TILE, within_ref.shape[1:]
    at = 0
    for column in range(shape[0]):
        own = column // TILE
        for t in range(own, count):
            weights = jnp.broadcast_to(
                low_ref[t * TILE : (t + 1) * TILE, column : column + 1], tile
            )
            if t == own:
                within_ref[column] = weights
            else:
                after_ref[at] = weights
                at += 1


def sweep_kernel(within_ref, after_ref, pre_ref, scale_ref, *refs):
    sums, out_ref = refs[:-1], refs[-1]
    rank, rows = pre_ref.shape
    total = sums[0][...]
    for ref in sums[1:]:
        total += ref[...]
    start = total.T * scale_ref[...] - pre_ref[...]
    count = rank // TILE
    tile = (TILE, rows)
    place = lax.broadcasted_iota(jnp.int32, tile, 0)
    rest = [start[t * TILE : (t + 1) * TILE] for t in range(count)]
    at = 0
    for k in range(count):
        wide = [jnp.broadcast_to(rest[k][s : s + 1], tile) for s in range(TILE)]
        for s in range(TILE):
            done = wide[s] = jnp.maximum(wide[s], 0.0)
            column = k * TILE + s
            for t in range(s + 1, TILE):
                wide[t] = wide[t] - jnp.broadcast_to(within_ref[column, t : t + 1], tile) * done
            for t in range(k + 1, count):
                rest[t] = rest[t] - after_ref[at] * done
                at += 1
        rest[k] = wide[0]
        for s in range(1, TILE):
            rest[k] = jnp.where(place == s, wide[s], rest[k])
    out_ref[...] = jnp.concatenate(rest, 0).T


def body(blocks, coords, factor_a, factor_b, factor_c):
    n_grp = lax.axis_size("grp")
    n_rep = lax.axis_size("rep")
    n_x = n_grp // CORES
    near = 2 if n_rep % 2 == 0 else 1
    line = n_rep // near
    nblk = blocks.shape[0]
    rank = factor_a.shape[1]
    tiles = rank // TILE
    jb = factor_b.shape[0] // BS
    ab = factor_a.shape[0] // BS
    params = pltpu.CompilerParams(vmem_limit_bytes=16 * 2**20)

    def move(value, chips, swap, beside=0, along=0):
        def to(x, c, rep):
            to_rep = partner(rep // near, along, line) * near + ((rep + beside) % near)
            return (x + chips) % n_x, c ^ swap, to_rep

        return lax.ppermute(value, ("grp", "rep"), moves(n_grp, n_rep, to))

    asks = [move(coords, d, 1) for d in range(1, n_x)]
    mate_b = move(factor_b, 0, 1)
    mate_c = move(factor_c, 0, 1)
    own_b, own_c = pl.pallas_call(
        load_kernel,
        out_shape=[jax.ShapeDtypeStruct(factor_b.shape, factor_b.dtype)] * 2,
        in_specs=[HBM] * 2,
        out_specs=[VMEM] * 2,
        scratch_shapes=[pltpu.SemaphoreType.DMA((2,))],
        compiler_params=params,
        name="load_shards",
    )(
        pltpu.with_memory_space_constraint(factor_b, pltpu.HBM),
        pltpu.with_memory_space_constraint(factor_c, pltpu.HBM),
    )
    factors = (own_b, mate_b, own_c, mate_c)

    chip_gram = pl.pallas_call(
        gram_kernel,
        out_shape=jax.ShapeDtypeStruct((rank, rank), jnp.float32),
        in_specs=[VMEM] * 4,
        out_specs=VMEM,
        compiler_params=params,
        name="chip_gram",
    )(*factors)
    asks, chip_gram = lax.optimization_barrier((asks, chip_gram))

    answers = pl.pallas_call(
        functools.partial(gather_kernel, n_x - 1, nblk, jb),
        out_shape=[jax.ShapeDtypeStruct((2 * nblk, BS, rank), factor_b.dtype)] * (n_x - 1),
        in_specs=[SMEM] * (n_x - 1) + [VMEM] * 4,
        out_specs=[VMEM] * (n_x - 1),
        compiler_params=params,
        name="gather_rows",
    )(*asks, *factors)
    answers, chip_gram = lax.optimization_barrier((answers, chip_gram))
    found = [move(answers[d - 1], -d, 1) for d in range(1, n_x)]
    gram = chip_gram
    for d in range(1, n_x):
        gram = gram + move(chip_gram, d, 0)

    local = pl.pallas_call(
        functools.partial(local_kernel, n_x, nblk, jb),
        out_shape=[
            jax.ShapeDtypeStruct((2 * nblk, BS, rank), factor_b.dtype),
            jax.ShapeDtypeStruct((2 * nblk, TILE, rank), jnp.int32),
            jax.ShapeDtypeStruct((nblk, TILE, rank), jnp.float32),
        ],
        in_specs=[SMEM] + [VMEM] * 4,
        out_specs=[VMEM] * 3,
        compiler_params=params,
        name="local_rows",
    )(coords, *factors)
    found, local = lax.optimization_barrier((found, local))

    partial = pl.pallas_call(
        functools.partial(partial_kernel, n_x, nblk),
        out_shape=jax.ShapeDtypeStruct((nblk, BS + TILE, rank), jnp.float32),
        in_specs=[VMEM] * (3 + n_x),
        out_specs=VMEM,
        compiler_params=params,
        name="block_products",
    )(*local, *found, blocks)
    others = [
        move(partial, d, 1, beside)
        for d in range(n_x)
        for beside in range(near)
        if d or beside
    ]
    prepared = pl.pallas_call(
        prepare_kernel,
        out_shape=[
            jax.ShapeDtypeStruct((rank, TILE, ab * BS), jnp.float32),
            jax.ShapeDtypeStruct((tiles * (tiles - 1) // 2 * TILE, TILE, ab * BS), jnp.float32),
            jax.ShapeDtypeStruct((rank, ab * BS), jnp.float32),
            jax.ShapeDtypeStruct((rank, ab * BS), jnp.float32),
        ],
        in_specs=[VMEM] * 3,
        out_specs=[VMEM] * 4,
        scratch_shapes=[pltpu.VMEM((rank, rank), jnp.float32)],
        compiler_params=params,
        name="prepare_sweep",
    )(gram, move(gram, 0, 1), factor_a)
    arrived = [partial, move(partial, 0, 1), *others, *(move(value, 0, 1) for value in others)]

    sums = pl.pallas_call(
        functools.partial(owner_kernel, n_rep, near, ab, len(arrived)),
        out_shape=[jax.ShapeDtypeStruct(factor_a.shape, jnp.float32)] * line,
        in_specs=[VMEM] * len(arrived),
        out_specs=[VMEM] * line,
        compiler_params=params,
        name="sum_by_owner",
    )(*arrived)
    sums = [sums[0]] + [move(sums[d], 0, 1, 0, d) for d in range(1, line)]

    return pl.pallas_call(
        sweep_kernel,
        out_shape=jax.ShapeDtypeStruct(factor_a.shape, jnp.float32),
        in_specs=[VMEM] * (4 + line),
        out_specs=VMEM,
        compiler_params=params,
        name="sweep",
    )(*prepared, *sums)


def solution(mesh):
    placed = (
        P(("grp", "rep"), None, None),
        P(("grp", "rep"), None),
        P(("grp", "rep"), None),
        P("grp", None),
        P("grp", None),
    )
    return jax.shard_map(
        body, mesh=mesh, in_specs=placed, out_specs=P(("grp", "rep"), None), check_vma=False
    )
```

```python
import functools

import jax
import jax.numpy as jnp
from jax import lax
from jax.experimental import pallas as pl
from jax.experimental.pallas import tpu as pltpu
from jax.sharding import PartitionSpec as P

BS = 64
TILE = 8
CORES = 2
EXACT = lax.Precision.HIGHEST
VMEM = pl.BlockSpec(memory_space=pltpu.VMEM)
HBM = pl.BlockSpec(memory_space=pltpu.HBM)


def moves(n_grp, n_rep, to):
    pairs = []
    for g in range(n_grp):
        for rep in range(n_rep):
            x, c, to_rep = to(g // CORES, g % CORES, rep)
            pairs.append((g * n_rep + rep, (x * CORES + c) * n_rep + to_rep))
    return pairs


def partner(index, offset, size):
    return index ^ offset if size & (size - 1) == 0 else (index + offset) % size


def here():
    grp = lax.axis_index("grp")
    return lax.div(grp, CORES), lax.rem(grp, CORES), lax.axis_index("rep")


def load_kernel(b_ref, c_ref, own_b, own_c, sems):
    copies = [
        pltpu.make_async_copy(src, dst, sems.at[i])
        for i, (src, dst) in enumerate(((b_ref, own_b), (c_ref, own_c)))
    ]
    for copy in copies:
        copy.start()
    for copy in copies:
        copy.wait()


def gram_kernel(own_b, mate_b, own_c, mate_c, out_ref):
    dims = (((0,), (0,)), ((), ()))
    for mode, shards in enumerate(((own_b, mate_b), (own_c, mate_c))):
        total = 0.0
        for ref in shards:
            total += lax.dot_general(ref[...], ref[...], dims, preferred_element_type=jnp.float32)
        out_ref[mode] = total


def row_block(own, mate, local, core, jb):
    row = pl.multiple_of(lax.rem(local, jb) * BS, BS)
    return jnp.where(lax.div(local, jb) == core, own[pl.ds(row, BS)], mate[pl.ds(row, BS)])


def gather_kernel(n_ask, nblk, jb, *refs):
    asks, factors, outs = refs[:n_ask], refs[n_ask : n_ask + 4], refs[n_ask + 4 :]
    _, core, _ = here()
    for ask, out in zip(asks, outs):
        for mode in range(2):
            for n in range(nblk):
                local = lax.rem(ask[...][n, 1 + mode], CORES * jb)
                out[mode * nblk + n] = row_block(*factors[2 * mode : 2 * mode + 2], local, core, jb)


def local_kernel(n_x, nblk, jb, ask_ref, *refs):
    factors, (rows_ref, far_ref, first_ref) = refs[:4], refs[4:]
    ask = ask_ref[...]
    my_x, core, _ = here()
    for mode in range(2):
        for n in range(nblk):
            slot = mode * nblk + n
            wanted = ask[n, 1 + mode]
            local = lax.rem(wanted, CORES * jb)
            rows_ref[slot] = row_block(*factors[2 * mode : 2 * mode + 2], local, core, jb)
            far = lax.rem(lax.div(wanted, CORES * jb) - my_x + n_x, n_x)
            far_ref[slot] = jnp.full(far_ref.shape[1:], far, jnp.int32)
    place = lax.broadcasted_iota(jnp.int32, first_ref.shape, 0)
    first = jnp.zeros(first_ref.shape, jnp.int32)
    for n in range(nblk):
        first = jnp.where(place == n, ask[n, 0], first)
    first_ref[...] = first.astype(jnp.float32)


def partial_kernel(n_x, nblk, rows_ref, far_ref, first_ref, *refs):
    found, blocks_ref, out_ref = refs[:-2], refs[-2], refs[-1]

    def rows_of(n, mode):
        slot = mode * nblk + n
        rows = rows_ref[slot].astype(jnp.float32)
        for d in range(1, n_x):
            rows = jnp.where(far_ref[slot, :1] == d, found[d - 1][slot].astype(jnp.float32), rows)
        return rows

    step = 8
    for n in range(nblk):
        left, right = rows_of(n, 0), rows_of(n, 1)
        rank = left.shape[1]
        total = jnp.zeros((BS, rank), jnp.float32)
        for j in range(0, BS, step):
            khatri = (left[j : j + step, None, :] * right[None, :, :]).astype(jnp.bfloat16)
            total += jnp.dot(
                blocks_ref[n, :, j * BS : (j + step) * BS],
                khatri.reshape(step * BS, rank),
                preferred_element_type=jnp.float32,
            )
        out_ref[n * BS : (n + 1) * BS] = total
    out_ref[nblk * BS :] = first_ref[...]


def owner_kernel(nblk, n_rep, near, ab, count, *refs):
    arrived, outs = refs[:count], refs[count:]
    my_x, core, rep = here()
    line = n_rep // near
    at, side = lax.div(rep, near), lax.rem(rep, near)
    for offset, out in enumerate(outs):
        if line & (line - 1) == 0:
            to_at = lax.bitwise_xor(at, offset)
        else:
            to_at = lax.rem(at + offset, line)
        to_core = core if offset == 0 else 1 - core
        first = ((my_x * CORES + to_core) * n_rep + to_at * near + side) * ab
        for sub in range(ab):
            target = (first + sub).astype(jnp.float32)
            total = None
            for ref in arrived:
                for n in range(nblk):
                    at_id = nblk * BS + n
                    term = jnp.where(
                        ref[at_id : at_id + 1] == target, ref[n * BS : (n + 1) * BS], 0.0
                    )
                    total = term if total is None else total + term
            out[sub * BS : (sub + 1) * BS] = total


def prepare_kernel(n_x, *refs):
    grams = refs[:n_x]
    a_ref, within_ref, after_ref, pre_ref, scale_ref, low_ref = refs[n_x:]
    gram_b, gram_c = grams[0][0], grams[0][1]
    for ref in grams[1:]:
        gram_b += ref[0]
        gram_c += ref[1]
    shape = gram_b.shape
    at_row = lax.broadcasted_iota(jnp.int32, shape, 0)
    at_col = lax.broadcasted_iota(jnp.int32, shape, 1)

    def diagonal(square, axis):
        return jnp.sum(jnp.where(at_row == at_col, square, 0.0), axis=axis, keepdims=True)

    norm_b_row, norm_b_col = jnp.sqrt(diagonal(gram_b, 0)), jnp.sqrt(diagonal(gram_b, 1))
    norm_c_row, norm_c_col = jnp.sqrt(diagonal(gram_c, 0)), jnp.sqrt(diagonal(gram_c, 1))
    gram = gram_b / (norm_b_col * norm_b_row) * (gram_c / (norm_c_col * norm_c_row))
    pivot = diagonal(gram, 1)
    steps = gram.T / pivot
    low_ref[...] = jnp.where(at_col < at_row, steps, 0.0)
    later = jnp.where(at_col > at_row, steps, 0.0)
    pre_ref[...] = lax.dot_general(
        later, a_ref[...], (((1,), (1,)), ((), ())), precision=EXACT, preferred_element_type=jnp.float32
    )
    scale_ref[...] = jnp.broadcast_to(1.0 / (norm_b_col * norm_c_col * pivot), scale_ref.shape)
    count, tile = shape[0] // TILE, within_ref.shape[1:]
    at = 0
    for column in range(shape[0]):
        own = column // TILE
        for t in range(own, count):
            weights = jnp.broadcast_to(
                low_ref[t * TILE : (t + 1) * TILE, column : column + 1], tile
            )
            if t == own:
                within_ref[column] = weights
            else:
                after_ref[at] = weights
                at += 1


def sweep_kernel(within_ref, after_ref, pre_ref, scale_ref, *refs):
    sums, out_ref = refs[:-1], refs[-1]
    rank, rows = pre_ref.shape
    total = sums[0][...]
    for ref in sums[1:]:
        total += ref[...]
    start = total.T * scale_ref[...] - pre_ref[...]
    count = rank // TILE
    tile = (TILE, rows)
    place = lax.broadcasted_iota(jnp.int32, tile, 0)
    rest = [start[t * TILE : (t + 1) * TILE] for t in range(count)]
    at = 0
    for k in range(count):
        wide = [jnp.broadcast_to(rest[k][s : s + 1], tile) for s in range(TILE)]
        for s in range(TILE):
            done = wide[s] = jnp.maximum(wide[s], 0.0)
            column = k * TILE + s
            for t in range(s + 1, TILE):
                wide[t] = wide[t] - jnp.broadcast_to(within_ref[column, t : t + 1], tile) * done
            for t in range(k + 1, count):
                rest[t] = rest[t] - after_ref[at] * done
                at += 1
        rest[k] = wide[0]
        for s in range(1, TILE):
            rest[k] = jnp.where(place == s, wide[s], rest[k])
    out_ref[...] = jnp.concatenate(rest, 0).T


def body(blocks, coords, factor_a, factor_b, factor_c):
    n_grp = lax.axis_size("grp")
    n_rep = lax.axis_size("rep")
    n_x = n_grp // CORES
    near = 2 if n_rep % 2 == 0 else 1
    line = n_rep // near
    nblk = blocks.shape[0]
    rank = factor_a.shape[1]
    tiles = rank // TILE
    id_rows = -(-nblk // TILE) * TILE
    jb = factor_b.shape[0] // BS
    ab = factor_a.shape[0] // BS
    params = pltpu.CompilerParams(vmem_limit_bytes=16 * 2**20)

    def move(value, chips, swap, beside=0, along=0):
        def to(x, c, rep):
            to_rep = partner(rep // near, along, line) * near + ((rep + beside) % near)
            return (x + chips) % n_x, c ^ swap, to_rep

        return lax.ppermute(value, ("grp", "rep"), moves(n_grp, n_rep, to))

    asks = [move(coords, d, 1) for d in range(1, n_x)]
    mate_b = move(factor_b, 0, 1)
    mate_c = move(factor_c, 0, 1)
    own_b, own_c = pl.pallas_call(
        load_kernel,
        out_shape=[jax.ShapeDtypeStruct(factor_b.shape, factor_b.dtype)] * 2,
        in_specs=[HBM] * 2,
        out_specs=[VMEM] * 2,
        scratch_shapes=[pltpu.SemaphoreType.DMA((2,))],
        compiler_params=params,
        name="load_shards",
    )(
        pltpu.with_memory_space_constraint(factor_b, pltpu.HBM),
        pltpu.with_memory_space_constraint(factor_c, pltpu.HBM),
    )
    factors = (own_b, mate_b, own_c, mate_c)

    chip_gram = pl.pallas_call(
        gram_kernel,
        out_shape=jax.ShapeDtypeStruct((2, rank, rank), jnp.float32),
        in_specs=[VMEM] * 4,
        out_specs=VMEM,
        compiler_params=params,
        name="chip_gram",
    )(*factors)

    answers = pl.pallas_call(
        functools.partial(gather_kernel, n_x - 1, nblk, jb),
        out_shape=[jax.ShapeDtypeStruct((2 * nblk, BS, rank), factor_b.dtype)] * (n_x - 1),
        in_specs=[VMEM] * (n_x - 1) + [VMEM] * 4,
        out_specs=[VMEM] * (n_x - 1),
        compiler_params=params,
        name="gather_rows",
    )(*asks, *factors)
    answers, chip_gram = lax.optimization_barrier((answers, chip_gram))
    found = [move(answers[d - 1], -d, 1) for d in range(1, n_x)]
    grams = [chip_gram] + [move(chip_gram, d, 1) for d in range(1, n_x)]

    local = pl.pallas_call(
        functools.partial(local_kernel, n_x, nblk, jb),
        out_shape=[
            jax.ShapeDtypeStruct((2 * nblk, BS, rank), factor_b.dtype),
            jax.ShapeDtypeStruct((2 * nblk, TILE, rank), jnp.int32),
            jax.ShapeDtypeStruct((id_rows, rank), jnp.float32),
        ],
        in_specs=[VMEM] * 5,
        out_specs=[VMEM] * 3,
        compiler_params=params,
        name="local_rows",
    )(coords, *factors)
    found, local = lax.optimization_barrier((found, local))

    partial = pl.pallas_call(
        functools.partial(partial_kernel, n_x, nblk),
        out_shape=jax.ShapeDtypeStruct((nblk * BS + id_rows, rank), jnp.float32),
        in_specs=[VMEM] * (3 + n_x),
        out_specs=VMEM,
        compiler_params=params,
        name="block_products",
    )(*local, *found, blocks)
    others = [
        move(partial, d, 1, beside)
        for d in range(n_x)
        for beside in range(near)
        if d or beside
    ]
    prepared = pl.pallas_call(
        functools.partial(prepare_kernel, n_x),
        out_shape=[
            jax.ShapeDtypeStruct((rank, TILE, ab * BS), jnp.float32),
            jax.ShapeDtypeStruct((tiles * (tiles - 1) // 2 * TILE, TILE, ab * BS), jnp.float32),
            jax.ShapeDtypeStruct((rank, ab * BS), jnp.float32),
            jax.ShapeDtypeStruct((rank, ab * BS), jnp.float32),
        ],
        in_specs=[VMEM] * (n_x + 1),
        out_specs=[VMEM] * 4,
        scratch_shapes=[pltpu.VMEM((rank, rank), jnp.float32)],
        compiler_params=params,
        name="prepare_sweep",
    )(*grams, factor_a)
    arrived = [partial, move(partial, 0, 1), *others, *(move(value, 0, 1) for value in others)]

    sums = pl.pallas_call(
        functools.partial(owner_kernel, nblk, n_rep, near, ab, len(arrived)),
        out_shape=[jax.ShapeDtypeStruct(factor_a.shape, jnp.float32)] * line,
        in_specs=[VMEM] * len(arrived),
        out_specs=[VMEM] * line,
        compiler_params=params,
        name="sum_by_owner",
    )(*arrived)
    sums = [sums[0]] + [move(sums[d], 0, 1, 0, d) for d in range(line - 1, 0, -1)]

    return pl.pallas_call(
        sweep_kernel,
        out_shape=jax.ShapeDtypeStruct(factor_a.shape, jnp.float32),
        in_specs=[VMEM] * (4 + line),
        out_specs=VMEM,
        compiler_params=params,
        name="sweep",
    )(*prepared, *sums)


def solution(mesh):
    placed = (
        P(("grp", "rep"), None, None),
        P(("grp", "rep"), None),
        P(("grp", "rep"), None),
        P("grp", None),
        P("grp", None),
    )
    return jax.shard_map(
        body, mesh=mesh, in_specs=placed, out_specs=P(("grp", "rep"), None), check_vma=False
    )
```

```python
import functools

import jax
import jax.numpy as jnp
from jax import lax
from jax.experimental import pallas as pl
from jax.experimental.pallas import tpu as pltpu
from jax.sharding import PartitionSpec as P

BS = 64
TILE = 8
CORES = 2
EXACT = lax.Precision.HIGHEST
VMEM = pl.BlockSpec(memory_space=pltpu.VMEM)
HBM = pl.BlockSpec(memory_space=pltpu.HBM)


def moves(n_grp, n_rep, to):
    pairs = []
    for g in range(n_grp):
        for rep in range(n_rep):
            x, c, to_rep = to(g // CORES, g % CORES, rep)
            pairs.append((g * n_rep + rep, (x * CORES + c) * n_rep + to_rep))
    return pairs


def partner(index, offset, size):
    return index ^ offset if size & (size - 1) == 0 else (index + offset) % size


def here():
    grp = lax.axis_index("grp")
    return lax.div(grp, CORES), lax.rem(grp, CORES), lax.axis_index("rep")


def load_kernel(b_ref, c_ref, own_b, own_c, sems):
    copies = [
        pltpu.make_async_copy(src, dst, sems.at[i])
        for i, (src, dst) in enumerate(((b_ref, own_b), (c_ref, own_c)))
    ]
    for copy in copies:
        copy.start()
    for copy in copies:
        copy.wait()


def gram_kernel(own_b, mate_b, own_c, mate_c, out_ref):
    dims = (((0,), (0,)), ((), ()))
    for mode, shards in enumerate(((own_b, mate_b), (own_c, mate_c))):
        total = 0.0
        for ref in shards:
            total += lax.dot_general(ref[...], ref[...], dims, preferred_element_type=jnp.float32)
        out_ref[mode] = total


def row_block(own, mate, local, core, jb):
    row = pl.multiple_of(lax.rem(local, jb) * BS, BS)
    return jnp.where(lax.div(local, jb) == core, own[pl.ds(row, BS)], mate[pl.ds(row, BS)])


def gather_kernel(n_ask, nblk, jb, *refs):
    asks, factors, outs = refs[:n_ask], refs[n_ask : n_ask + 4], refs[n_ask + 4 :]
    _, core, _ = here()
    for ask, out in zip(asks, outs):
        for mode in range(2):
            for n in range(nblk):
                local = lax.rem(ask[...][n, 1 + mode], CORES * jb)
                out[mode * nblk + n] = row_block(*factors[2 * mode : 2 * mode + 2], local, core, jb)


def local_kernel(n_x, nblk, jb, ask_ref, *refs):
    factors, (rows_ref, far_ref, first_ref) = refs[:4], refs[4:]
    ask = ask_ref[...]
    my_x, core, _ = here()
    for mode in range(2):
        for n in range(nblk):
            slot = mode * nblk + n
            wanted = ask[n, 1 + mode]
            local = lax.rem(wanted, CORES * jb)
            rows_ref[slot] = row_block(*factors[2 * mode : 2 * mode + 2], local, core, jb)
            far = lax.rem(lax.div(wanted, CORES * jb) - my_x + n_x, n_x)
            far_ref[slot] = jnp.full(far_ref.shape[1:], far, jnp.int32)
    place = lax.broadcasted_iota(jnp.int32, first_ref.shape, 0)
    first = jnp.zeros(first_ref.shape, jnp.int32)
    for n in range(nblk):
        first = jnp.where(place == n, ask[n, 0], first)
    first_ref[...] = first.astype(jnp.float32)


def partial_kernel(n_x, nblk, rows_ref, far_ref, first_ref, *refs):
    found, blocks_ref, out_ref = refs[:-2], refs[-2], refs[-1]

    def rows_of(n, mode):
        slot = mode * nblk + n
        rows = rows_ref[slot].astype(jnp.float32)
        for d in range(1, n_x):
            rows = jnp.where(far_ref[slot, :1] == d, found[d - 1][slot].astype(jnp.float32), rows)
        return rows

    step = 8
    for n in range(nblk):
        left, right = rows_of(n, 0), rows_of(n, 1)
        rank = left.shape[1]
        total = jnp.zeros((BS, rank), jnp.float32)
        for j in range(0, BS, step):
            khatri = (left[j : j + step, None, :] * right[None, :, :]).astype(jnp.bfloat16)
            total += jnp.dot(
                blocks_ref[n, :, j * BS : (j + step) * BS],
                khatri.reshape(step * BS, rank),
                preferred_element_type=jnp.float32,
            )
        out_ref[n * BS : (n + 1) * BS] = total
    out_ref[nblk * BS :] = first_ref[...]


def owner_kernel(nblk, n_rep, near, ab, count, *refs):
    arrived, outs = refs[:count], refs[count:]
    my_x, core, rep = here()
    line = n_rep // near
    at, side = lax.div(rep, near), lax.rem(rep, near)
    for offset, out in enumerate(outs):
        if line & (line - 1) == 0:
            to_at = lax.bitwise_xor(at, offset)
        else:
            to_at = lax.rem(at + offset, line)
        to_core = core if offset == 0 else 1 - core
        first = ((my_x * CORES + to_core) * n_rep + to_at * near + side) * ab
        for sub in range(ab):
            target = (first + sub).astype(jnp.float32)
            total = None
            for ref in arrived:
                for n in range(nblk):
                    at_id = nblk * BS + n
                    term = jnp.where(
                        ref[at_id : at_id + 1] == target, ref[n * BS : (n + 1) * BS], 0.0
                    )
                    total = term if total is None else total + term
            out[sub * BS : (sub + 1) * BS] = total


def prepare_kernel(n_x, *refs):
    grams = refs[:n_x]
    a_ref, within_ref, after_ref, pre_ref, scale_ref, low_ref = refs[n_x:]
    gram_b, gram_c = grams[0][0], grams[0][1]
    for ref in grams[1:]:
        gram_b += ref[0]
        gram_c += ref[1]
    shape = gram_b.shape
    at_row = lax.broadcasted_iota(jnp.int32, shape, 0)
    at_col = lax.broadcasted_iota(jnp.int32, shape, 1)

    def diagonal(square, axis):
        return jnp.sum(jnp.where(at_row == at_col, square, 0.0), axis=axis, keepdims=True)

    norm_b_row, norm_b_col = jnp.sqrt(diagonal(gram_b, 0)), jnp.sqrt(diagonal(gram_b, 1))
    norm_c_row, norm_c_col = jnp.sqrt(diagonal(gram_c, 0)), jnp.sqrt(diagonal(gram_c, 1))
    gram = gram_b / (norm_b_col * norm_b_row) * (gram_c / (norm_c_col * norm_c_row))
    pivot = diagonal(gram, 1)
    steps = gram.T / pivot
    low_ref[...] = jnp.where(at_col < at_row, steps, 0.0)
    later = jnp.where(at_col > at_row, steps, 0.0)
    pre_ref[...] = lax.dot_general(
        later, a_ref[...], (((1,), (1,)), ((), ())), precision=EXACT, preferred_element_type=jnp.float32
    )
    scale_ref[...] = jnp.broadcast_to(1.0 / (norm_b_col * norm_c_col * pivot), scale_ref.shape)
    count, tile = shape[0] // TILE, within_ref.shape[1:]
    at = 0
    for column in range(shape[0]):
        own = column // TILE
        for t in range(own, count):
            weights = jnp.broadcast_to(
                low_ref[t * TILE : (t + 1) * TILE, column : column + 1], tile
            )
            if t == own:
                within_ref[column] = weights
            else:
                after_ref[at] = weights
                at += 1


def sweep_kernel(within_ref, after_ref, pre_ref, scale_ref, *refs):
    sums, out_ref = refs[:-1], refs[-1]
    rank, rows = pre_ref.shape
    total = sums[0][...]
    for ref in sums[1:]:
        total += ref[...]
    start = total.T * scale_ref[...] - pre_ref[...]
    count = rank // TILE
    tile = (TILE, rows)
    place = lax.broadcasted_iota(jnp.int32, tile, 0)
    rest = [start[t * TILE : (t + 1) * TILE] for t in range(count)]
    at = 0
    for k in range(count):
        wide = [jnp.broadcast_to(rest[k][s : s + 1], tile) for s in range(TILE)]
        for s in range(TILE):
            done = wide[s] = jnp.maximum(wide[s], 0.0)
            column = k * TILE + s
            for t in range(s + 1, TILE):
                wide[t] = wide[t] - jnp.broadcast_to(within_ref[column, t : t + 1], tile) * done
            for t in range(k + 1, count):
                rest[t] = rest[t] - after_ref[at] * done
                at += 1
        rest[k] = wide[0]
        for s in range(1, TILE):
            rest[k] = jnp.where(place == s, wide[s], rest[k])
    out_ref[...] = jnp.concatenate(rest, 0).T


def body(blocks, coords, factor_a, factor_b, factor_c):
    n_grp = lax.axis_size("grp")
    n_rep = lax.axis_size("rep")
    n_x = n_grp // CORES
    near = 2 if n_rep % 2 == 0 else 1
    line = n_rep // near
    nblk = blocks.shape[0]
    rank = factor_a.shape[1]
    tiles = rank // TILE
    id_rows = -(-nblk // TILE) * TILE
    jb = factor_b.shape[0] // BS
    ab = factor_a.shape[0] // BS
    params = pltpu.CompilerParams(vmem_limit_bytes=16 * 2**20)

    def move(value, chips, swap, beside=0, along=0):
        def to(x, c, rep):
            to_rep = partner(rep // near, along, line) * near + ((rep + beside) % near)
            return (x + chips) % n_x, c ^ swap, to_rep

        return lax.ppermute(value, ("grp", "rep"), moves(n_grp, n_rep, to))

    asks = [move(coords, d, 1) for d in range(1, n_x)]
    mate_b = move(factor_b, 0, 1)
    mate_c = move(factor_c, 0, 1)
    own_b, own_c = pl.pallas_call(
        load_kernel,
        out_shape=[jax.ShapeDtypeStruct(factor_b.shape, factor_b.dtype)] * 2,
        in_specs=[HBM] * 2,
        out_specs=[VMEM] * 2,
        scratch_shapes=[pltpu.SemaphoreType.DMA((2,))],
        compiler_params=params,
        name="load_shards",
    )(
        pltpu.with_memory_space_constraint(factor_b, pltpu.HBM),
        pltpu.with_memory_space_constraint(factor_c, pltpu.HBM),
    )
    factors = (own_b, mate_b, own_c, mate_c)

    chip_gram = pl.pallas_call(
        gram_kernel,
        out_shape=jax.ShapeDtypeStruct((2, rank, rank), jnp.float32),
        in_specs=[VMEM] * 4,
        out_specs=VMEM,
        compiler_params=params,
        name="chip_gram",
    )(*factors)

    answers = pl.pallas_call(
        functools.partial(gather_kernel, n_x - 1, nblk, jb),
        out_shape=[jax.ShapeDtypeStruct((2 * nblk, BS, rank), factor_b.dtype)] * (n_x - 1),
        in_specs=[VMEM] * (n_x - 1) + [VMEM] * 4,
        out_specs=[VMEM] * (n_x - 1),
        compiler_params=params,
        name="gather_rows",
    )(*asks, *factors)
    answers, chip_gram = lax.optimization_barrier((answers, chip_gram))
    found = [move(answers[d - 1], -d, 1) for d in range(1, n_x)]
    grams = [chip_gram] + [move(chip_gram, d, 1) for d in range(1, n_x)]

    local = pl.pallas_call(
        functools.partial(local_kernel, n_x, nblk, jb),
        out_shape=[
            jax.ShapeDtypeStruct((2 * nblk, BS, rank), factor_b.dtype),
            jax.ShapeDtypeStruct((2 * nblk, TILE, rank), jnp.int32),
            jax.ShapeDtypeStruct((id_rows, rank), jnp.float32),
        ],
        in_specs=[VMEM] * 5,
        out_specs=[VMEM] * 3,
        compiler_params=params,
        name="local_rows",
    )(coords, *factors)
    found, local = lax.optimization_barrier((found, local))

    partial = pl.pallas_call(
        functools.partial(partial_kernel, n_x, nblk),
        out_shape=jax.ShapeDtypeStruct((nblk * BS + id_rows, rank), jnp.float32),
        in_specs=[VMEM] * (3 + n_x),
        out_specs=VMEM,
        compiler_params=params,
        name="block_products",
    )(*local, *found, blocks)
    offsets = [(d, b) for d in range(n_x) for b in range(near) if d or b]

    def spread(value, pair):
        def to(x, c, rep):
            chips, beside = pair[(x + c + rep % near) % 2]
            to_rep = rep // near * near + (rep + beside) % near
            return (x + chips) % n_x, (c + chips + beside) % CORES, to_rep

        return lax.ppermute(value, ("grp", "rep"), moves(n_grp, n_rep, to))

    others = [spread(partial, pair) for pair in zip(offsets, reversed(offsets))]
    prepared = pl.pallas_call(
        functools.partial(prepare_kernel, n_x),
        out_shape=[
            jax.ShapeDtypeStruct((rank, TILE, ab * BS), jnp.float32),
            jax.ShapeDtypeStruct((tiles * (tiles - 1) // 2 * TILE, TILE, ab * BS), jnp.float32),
            jax.ShapeDtypeStruct((rank, ab * BS), jnp.float32),
            jax.ShapeDtypeStruct((rank, ab * BS), jnp.float32),
        ],
        in_specs=[VMEM] * (n_x + 1),
        out_specs=[VMEM] * 4,
        scratch_shapes=[pltpu.VMEM((rank, rank), jnp.float32)],
        compiler_params=params,
        name="prepare_sweep",
    )(*grams, factor_a)
    arrived = [partial, move(partial, 0, 1), *others, *(move(value, 0, 1) for value in others)]

    sums = pl.pallas_call(
        functools.partial(owner_kernel, nblk, n_rep, near, ab, len(arrived)),
        out_shape=[jax.ShapeDtypeStruct(factor_a.shape, jnp.float32)] * line,
        in_specs=[VMEM] * len(arrived),
        out_specs=[VMEM] * line,
        compiler_params=params,
        name="sum_by_owner",
    )(*arrived)
    sums = [sums[0]] + [move(sums[d], 0, 1, 0, d) for d in range(line - 1, 0, -1)]

    return pl.pallas_call(
        sweep_kernel,
        out_shape=jax.ShapeDtypeStruct(factor_a.shape, jnp.float32),
        in_specs=[VMEM] * (4 + line),
        out_specs=VMEM,
        compiler_params=params,
        name="sweep",
    )(*prepared, *sums)


def solution(mesh):
    placed = (
        P(("grp", "rep"), None, None),
        P(("grp", "rep"), None),
        P(("grp", "rep"), None),
        P("grp", None),
        P("grp", None),
    )
    return jax.shard_map(
        body, mesh=mesh, in_specs=placed, out_specs=P(("grp", "rep"), None), check_vma=False
    )
```

```python
import functools

import jax
import jax.numpy as jnp
from jax import lax
from jax.experimental import pallas as pl
from jax.experimental.pallas import tpu as pltpu
from jax.sharding import PartitionSpec as P

BS = 64
TILE = 8
CORES = 2
EXACT = lax.Precision.HIGHEST
VMEM = pl.BlockSpec(memory_space=pltpu.VMEM)
HBM = pl.BlockSpec(memory_space=pltpu.HBM)


def moves(n_grp, n_rep, to):
    pairs = []
    for g in range(n_grp):
        for rep in range(n_rep):
            x, c, to_rep = to(g // CORES, g % CORES, rep)
            pairs.append((g * n_rep + rep, (x * CORES + c) * n_rep + to_rep))
    return pairs


def partner(index, offset, size):
    return index ^ offset if size & (size - 1) == 0 else (index + offset) % size


def here():
    grp = lax.axis_index("grp")
    return lax.div(grp, CORES), lax.rem(grp, CORES), lax.axis_index("rep")


def load_kernel(b_ref, c_ref, own_b, own_c, sems):
    copies = [
        pltpu.make_async_copy(src, dst, sems.at[i])
        for i, (src, dst) in enumerate(((b_ref, own_b), (c_ref, own_c)))
    ]
    for copy in copies:
        copy.start()
    for copy in copies:
        copy.wait()


def gram_kernel(own_b, mate_b, own_c, mate_c, out_ref):
    dims = (((0,), (0,)), ((), ()))
    for mode, shards in enumerate(((own_b, mate_b), (own_c, mate_c))):
        total = 0.0
        for ref in shards:
            total += lax.dot_general(ref[...], ref[...], dims, preferred_element_type=jnp.float32)
        out_ref[mode] = total


def row_block(own, mate, local, core, jb):
    row = pl.multiple_of(lax.rem(local, jb) * BS, BS)
    return jnp.where(lax.div(local, jb) == core, own[pl.ds(row, BS)], mate[pl.ds(row, BS)])


def gather_kernel(n_ask, nblk, jb, *refs):
    asks, factors, outs = refs[:n_ask], refs[n_ask : n_ask + 4], refs[n_ask + 4 :]
    _, core, _ = here()
    for ask, out in zip(asks, outs):
        for mode in range(2):
            for n in range(nblk):
                local = lax.rem(ask[...][n, 1 + mode], CORES * jb)
                out[mode * nblk + n] = row_block(*factors[2 * mode : 2 * mode + 2], local, core, jb)


def local_kernel(n_x, nblk, jb, ask_ref, *refs):
    factors, (rows_ref, far_ref, first_ref) = refs[:4], refs[4:]
    ask = ask_ref[...]
    my_x, core, _ = here()
    for mode in range(2):
        for n in range(nblk):
            slot = mode * nblk + n
            wanted = ask[n, 1 + mode]
            local = lax.rem(wanted, CORES * jb)
            rows_ref[slot] = row_block(*factors[2 * mode : 2 * mode + 2], local, core, jb)
            far = lax.rem(lax.div(wanted, CORES * jb) - my_x + n_x, n_x)
            far_ref[slot] = jnp.full(far_ref.shape[1:], far, jnp.int32)
    place = lax.broadcasted_iota(jnp.int32, first_ref.shape, 0)
    first = jnp.zeros(first_ref.shape, jnp.int32)
    for n in range(nblk):
        first = jnp.where(place == n, ask[n, 0], first)
    first_ref[...] = first.astype(jnp.float32)


def partial_kernel(n_x, nblk, rows_ref, far_ref, first_ref, *refs):
    found, blocks_ref, out_ref = refs[:-2], refs[-2], refs[-1]

    def rows_of(n, mode):
        slot = mode * nblk + n
        rows = rows_ref[slot]
        for d in range(1, n_x):
            rows = jnp.where(far_ref[slot, :1] == d, found[d - 1][slot], rows)
        return rows

    step = 8
    for n in range(nblk):
        left, right = rows_of(n, 0), rows_of(n, 1)
        rank = left.shape[1]
        total = jnp.zeros((BS, rank), jnp.float32)
        for j in range(0, BS, step):
            khatri = left[j : j + step, None, :] * right[None, :, :]
            total += jnp.dot(
                blocks_ref[n, :, j * BS : (j + step) * BS],
                khatri.reshape(step * BS, rank),
                preferred_element_type=jnp.float32,
            )
        out_ref[n * BS : (n + 1) * BS] = total
    out_ref[nblk * BS :] = first_ref[...]


def owner_kernel(nblk, n_rep, near, ab, count, *refs):
    arrived, outs = refs[:count], refs[count:]
    my_x, core, rep = here()
    line = n_rep // near
    at, side = lax.div(rep, near), lax.rem(rep, near)
    for offset, out in enumerate(outs):
        if line & (line - 1) == 0:
            to_at = lax.bitwise_xor(at, offset)
        else:
            to_at = lax.rem(at + offset, line)
        to_core = core if offset == 0 else 1 - core
        first = ((my_x * CORES + to_core) * n_rep + to_at * near + side) * ab
        for sub in range(ab):
            target = (first + sub).astype(jnp.float32)
            total = None
            for ref in arrived:
                for n in range(nblk):
                    at_id = nblk * BS + n
                    term = jnp.where(
                        ref[at_id : at_id + 1] == target, ref[n * BS : (n + 1) * BS], 0.0
                    )
                    total = term if total is None else total + term
            out[sub * BS : (sub + 1) * BS] = total


def prepare_kernel(n_x, *refs):
    grams = refs[:n_x]
    a_ref, within_ref, after_ref, pre_ref, scale_ref, low_ref = refs[n_x:]
    gram_b, gram_c = grams[0][0], grams[0][1]
    for ref in grams[1:]:
        gram_b += ref[0]
        gram_c += ref[1]
    shape = gram_b.shape
    at_row = lax.broadcasted_iota(jnp.int32, shape, 0)
    at_col = lax.broadcasted_iota(jnp.int32, shape, 1)

    def diagonal(square, axis):
        return jnp.sum(jnp.where(at_row == at_col, square, 0.0), axis=axis, keepdims=True)

    norm_b_row, norm_b_col = jnp.sqrt(diagonal(gram_b, 0)), jnp.sqrt(diagonal(gram_b, 1))
    norm_c_row, norm_c_col = jnp.sqrt(diagonal(gram_c, 0)), jnp.sqrt(diagonal(gram_c, 1))
    gram = gram_b / (norm_b_col * norm_b_row) * (gram_c / (norm_c_col * norm_c_row))
    pivot = diagonal(gram, 1)
    steps = gram.T / pivot
    low_ref[...] = jnp.where(at_col < at_row, steps, 0.0)
    later = jnp.where(at_col > at_row, steps, 0.0)
    pre_ref[...] = lax.dot_general(
        later, a_ref[...], (((1,), (1,)), ((), ())), precision=EXACT, preferred_element_type=jnp.float32
    )
    scale_ref[...] = jnp.broadcast_to(1.0 / (norm_b_col * norm_c_col * pivot), scale_ref.shape)
    count, tile = shape[0] // TILE, within_ref.shape[1:]
    at = 0
    for column in range(shape[0]):
        own = column // TILE
        for t in range(own, count):
            weights = jnp.broadcast_to(
                low_ref[t * TILE : (t + 1) * TILE, column : column + 1], tile
            )
            if t == own:
                within_ref[column] = weights
            else:
                after_ref[at] = weights
                at += 1


def sweep_kernel(within_ref, after_ref, pre_ref, scale_ref, *refs):
    sums, out_ref = refs[:-1], refs[-1]
    rank, rows = pre_ref.shape
    total = sums[0][...]
    for ref in sums[1:]:
        total += ref[...]
    start = total.T * scale_ref[...] - pre_ref[...]
    count = rank // TILE
    tile = (TILE, rows)
    place = lax.broadcasted_iota(jnp.int32, tile, 0)
    rest = [start[t * TILE : (t + 1) * TILE] for t in range(count)]
    at = 0
    for k in range(count):
        wide = [jnp.broadcast_to(rest[k][s : s + 1], tile) for s in range(TILE)]
        for s in range(TILE):
            done = wide[s] = jnp.maximum(wide[s], 0.0)
            column = k * TILE + s
            for t in range(s + 1, TILE):
                wide[t] = wide[t] - jnp.broadcast_to(within_ref[column, t : t + 1], tile) * done
            for t in range(k + 1, count):
                rest[t] = rest[t] - after_ref[at] * done
                at += 1
        rest[k] = wide[0]
        for s in range(1, TILE):
            rest[k] = jnp.where(place == s, wide[s], rest[k])
    out_ref[...] = jnp.concatenate(rest, 0).T


def body(blocks, coords, factor_a, factor_b, factor_c):
    n_grp = lax.axis_size("grp")
    n_rep = lax.axis_size("rep")
    n_x = n_grp // CORES
    near = 2 if n_rep % 2 == 0 else 1
    line = n_rep // near
    nblk = blocks.shape[0]
    rank = factor_a.shape[1]
    tiles = rank // TILE
    id_rows = -(-nblk // TILE) * TILE
    jb = factor_b.shape[0] // BS
    ab = factor_a.shape[0] // BS
    params = pltpu.CompilerParams(vmem_limit_bytes=16 * 2**20)

    def move(value, chips, swap, beside=0, along=0):
        def to(x, c, rep):
            to_rep = partner(rep // near, along, line) * near + ((rep + beside) % near)
            return (x + chips) % n_x, c ^ swap, to_rep

        return lax.ppermute(value, ("grp", "rep"), moves(n_grp, n_rep, to))

    asks = [move(coords, d, 1) for d in range(1, n_x)]
    mate_b = move(factor_b, 0, 1)
    mate_c = move(factor_c, 0, 1)
    own_b, own_c = pl.pallas_call(
        load_kernel,
        out_shape=[jax.ShapeDtypeStruct(factor_b.shape, factor_b.dtype)] * 2,
        in_specs=[HBM] * 2,
        out_specs=[VMEM] * 2,
        scratch_shapes=[pltpu.SemaphoreType.DMA((2,))],
        compiler_params=params,
        name="load_shards",
    )(
        pltpu.with_memory_space_constraint(factor_b, pltpu.HBM),
        pltpu.with_memory_space_constraint(factor_c, pltpu.HBM),
    )
    factors = (own_b, mate_b, own_c, mate_c)

    chip_gram = pl.pallas_call(
        gram_kernel,
        out_shape=jax.ShapeDtypeStruct((2, rank, rank), jnp.float32),
        in_specs=[VMEM] * 4,
        out_specs=VMEM,
        compiler_params=params,
        name="chip_gram",
    )(*factors)

    answers = pl.pallas_call(
        functools.partial(gather_kernel, n_x - 1, nblk, jb),
        out_shape=[jax.ShapeDtypeStruct((2 * nblk, BS, rank), factor_b.dtype)] * (n_x - 1),
        in_specs=[VMEM] * (n_x - 1) + [VMEM] * 4,
        out_specs=[VMEM] * (n_x - 1),
        compiler_params=params,
        name="gather_rows",
    )(*asks, *factors)
    answers, chip_gram = lax.optimization_barrier((answers, chip_gram))
    found = [move(answers[d - 1], -d, 1) for d in range(1, n_x)]
    grams = [chip_gram] + [move(chip_gram, d, 1) for d in range(1, n_x)]

    local = pl.pallas_call(
        functools.partial(local_kernel, n_x, nblk, jb),
        out_shape=[
            jax.ShapeDtypeStruct((2 * nblk, BS, rank), factor_b.dtype),
            jax.ShapeDtypeStruct((2 * nblk, TILE, rank), jnp.int32),
            jax.ShapeDtypeStruct((id_rows, rank), jnp.float32),
        ],
        in_specs=[VMEM] * 5,
        out_specs=[VMEM] * 3,
        compiler_params=params,
        name="local_rows",
    )(coords, *factors)
    found, local = lax.optimization_barrier((found, local))

    partial = pl.pallas_call(
        functools.partial(partial_kernel, n_x, nblk),
        out_shape=jax.ShapeDtypeStruct((nblk * BS + id_rows, rank), jnp.float32),
        in_specs=[VMEM] * (3 + n_x),
        out_specs=VMEM,
        compiler_params=params,
        name="block_products",
    )(*local, *found, blocks)
    offsets = [(d, b) for d in range(n_x) for b in range(near) if d or b]

    def spread(value, pair):
        def to(x, c, rep):
            chips, beside = pair[(x + c + rep % near) % 2]
            to_rep = rep // near * near + (rep + beside) % near
            return (x + chips) % n_x, (c + chips + beside) % CORES, to_rep

        return lax.ppermute(value, ("grp", "rep"), moves(n_grp, n_rep, to))

    others = [spread(partial, pair) for pair in zip(offsets, reversed(offsets))]
    prepared = pl.pallas_call(
        functools.partial(prepare_kernel, n_x),
        out_shape=[
            jax.ShapeDtypeStruct((rank, TILE, ab * BS), jnp.float32),
            jax.ShapeDtypeStruct((tiles * (tiles - 1) // 2 * TILE, TILE, ab * BS), jnp.float32),
            jax.ShapeDtypeStruct((rank, ab * BS), jnp.float32),
            jax.ShapeDtypeStruct((rank, ab * BS), jnp.float32),
        ],
        in_specs=[VMEM] * (n_x + 1),
        out_specs=[VMEM] * 4,
        scratch_shapes=[pltpu.VMEM((rank, rank), jnp.float32)],
        compiler_params=params,
        name="prepare_sweep",
    )(*grams, factor_a)
    arrived = [partial, move(partial, 0, 1), *others, *(move(value, 0, 1) for value in others)]

    sums = pl.pallas_call(
        functools.partial(owner_kernel, nblk, n_rep, near, ab, len(arrived)),
        out_shape=[jax.ShapeDtypeStruct(factor_a.shape, jnp.float32)] * line,
        in_specs=[VMEM] * len(arrived),
        out_specs=[VMEM] * line,
        compiler_params=params,
        name="sum_by_owner",
    )(*arrived)
    sums = [sums[0]] + [move(sums[d], 0, 1, 0, d) for d in range(line - 1, 0, -1)]

    return pl.pallas_call(
        sweep_kernel,
        out_shape=jax.ShapeDtypeStruct(factor_a.shape, jnp.float32),
        in_specs=[VMEM] * (4 + line),
        out_specs=VMEM,
        compiler_params=params,
        name="sweep",
    )(*prepared, *sums)


def solution(mesh):
    placed = (
        P(("grp", "rep"), None, None),
        P(("grp", "rep"), None),
        P(("grp", "rep"), None),
        P("grp", None),
        P("grp", None),
    )
    return jax.shard_map(
        body, mesh=mesh, in_specs=placed, out_specs=P(("grp", "rep"), None), check_vma=False
    )
```

```python
import functools

import jax
import jax.numpy as jnp
from jax import lax
from jax.experimental import pallas as pl
from jax.experimental.pallas import tpu as pltpu
from jax.sharding import PartitionSpec as P

BS = 64
TILE = 8
CORES = 2
EXACT = lax.Precision.HIGHEST
VMEM = pl.BlockSpec(memory_space=pltpu.VMEM)
HBM = pl.BlockSpec(memory_space=pltpu.HBM)


def moves(n_grp, n_rep, to):
    pairs = []
    for g in range(n_grp):
        for rep in range(n_rep):
            x, c, to_rep = to(g // CORES, g % CORES, rep)
            pairs.append((g * n_rep + rep, (x * CORES + c) * n_rep + to_rep))
    return pairs


def partner(index, offset, size):
    return index ^ offset if size & (size - 1) == 0 else (index + offset) % size


def here():
    grp = lax.axis_index("grp")
    return lax.div(grp, CORES), lax.rem(grp, CORES), lax.axis_index("rep")


def load_kernel(b_ref, c_ref, own_b, own_c, sems):
    copies = [
        pltpu.make_async_copy(src, dst, sems.at[i])
        for i, (src, dst) in enumerate(((b_ref, own_b), (c_ref, own_c)))
    ]
    for copy in copies:
        copy.start()
    for copy in copies:
        copy.wait()


def gram_kernel(own_b, mate_b, own_c, mate_c, out_ref):
    dims = (((0,), (0,)), ((), ()))
    for mode, shards in enumerate(((own_b, mate_b), (own_c, mate_c))):
        total = 0.0
        for ref in shards:
            total += lax.dot_general(ref[...], ref[...], dims, preferred_element_type=jnp.float32)
        out_ref[mode] = total


def row_block(own, mate, local, core, jb):
    row = pl.multiple_of(lax.rem(local, jb) * BS, BS)
    return jnp.where(lax.div(local, jb) == core, own[pl.ds(row, BS)], mate[pl.ds(row, BS)])


def gather_kernel(n_ask, nblk, jb, *refs):
    asks, factors, outs = refs[:n_ask], refs[n_ask : n_ask + 4], refs[n_ask + 4 :]
    _, core, _ = here()
    for ask, out in zip(asks, outs):
        for mode in range(2):
            for n in range(nblk):
                local = lax.rem(ask[...][n, 1 + mode], CORES * jb)
                out[mode * nblk + n] = row_block(*factors[2 * mode : 2 * mode + 2], local, core, jb)


def local_kernel(n_x, nblk, jb, ask_ref, *refs):
    factors, (rows_ref, far_ref, first_ref) = refs[:4], refs[4:]
    ask = ask_ref[...]
    my_x, core, _ = here()
    for mode in range(2):
        for n in range(nblk):
            slot = mode * nblk + n
            wanted = ask[n, 1 + mode]
            local = lax.rem(wanted, CORES * jb)
            rows_ref[slot] = row_block(*factors[2 * mode : 2 * mode + 2], local, core, jb)
            far = lax.rem(lax.div(wanted, CORES * jb) - my_x + n_x, n_x)
            far_ref[slot] = jnp.full(far_ref.shape[1:], far, jnp.int32)
    place = lax.broadcasted_iota(jnp.int32, first_ref.shape, 0)
    first = jnp.zeros(first_ref.shape, jnp.int32)
    for n in range(nblk):
        first = jnp.where(place == n, ask[n, 0], first)
    first_ref[...] = first.astype(jnp.float32)


def partial_kernel(n_x, nblk, rows_ref, far_ref, first_ref, *refs):
    found, blocks_ref, out_ref = refs[:-2], refs[-2], refs[-1]

    def rows_of(n, mode):
        slot = mode * nblk + n
        rows = rows_ref[slot]
        for d in range(1, n_x):
            rows = jnp.where(far_ref[slot, :1] == d, found[d - 1][slot], rows)
        return rows

    step = 8
    for n in range(nblk):
        left, right = rows_of(n, 0), rows_of(n, 1)
        rank = left.shape[1]
        total = jnp.zeros((BS, rank), jnp.float32)
        for j in range(0, BS, step):
            khatri = left[j : j + step, None, :] * right[None, :, :]
            total += jnp.dot(
                blocks_ref[n, :, j * BS : (j + step) * BS],
                khatri.reshape(step * BS, rank),
                preferred_element_type=jnp.float32,
            )
        out_ref[n * BS : (n + 1) * BS] = total
    out_ref[nblk * BS :] = first_ref[...]


def owner_kernel(places, nblk, n_rep, near, ab, count, *refs):
    arrived, outs = refs[:count], refs[count:]
    my_x, core, rep = here()
    line = n_rep // near
    at, side = lax.div(rep, near), lax.rem(rep, near)
    for offset, out in zip(places, outs):
        if line & (line - 1) == 0:
            to_at = lax.bitwise_xor(at, offset)
        else:
            to_at = lax.rem(at + offset, line)
        to_core = core if offset == 0 else 1 - core
        first = ((my_x * CORES + to_core) * n_rep + to_at * near + side) * ab
        for sub in range(ab):
            target = (first + sub).astype(jnp.float32)
            total = None
            for ref in arrived:
                for n in range(nblk):
                    at_id = nblk * BS + n
                    term = jnp.where(
                        ref[at_id : at_id + 1] == target, ref[n * BS : (n + 1) * BS], 0.0
                    )
                    total = term if total is None else total + term
            out[sub * BS : (sub + 1) * BS] = total


def prepare_kernel(n_x, *refs):
    grams = refs[:n_x]
    a_ref, within_ref, after_ref, pre_ref, scale_ref, low_ref = refs[n_x:]
    gram_b, gram_c = grams[0][0], grams[0][1]
    for ref in grams[1:]:
        gram_b += ref[0]
        gram_c += ref[1]
    shape = gram_b.shape
    at_row = lax.broadcasted_iota(jnp.int32, shape, 0)
    at_col = lax.broadcasted_iota(jnp.int32, shape, 1)

    def diagonal(square, axis):
        return jnp.sum(jnp.where(at_row == at_col, square, 0.0), axis=axis, keepdims=True)

    norm_b_row, norm_b_col = jnp.sqrt(diagonal(gram_b, 0)), jnp.sqrt(diagonal(gram_b, 1))
    norm_c_row, norm_c_col = jnp.sqrt(diagonal(gram_c, 0)), jnp.sqrt(diagonal(gram_c, 1))
    gram = gram_b / (norm_b_col * norm_b_row) * (gram_c / (norm_c_col * norm_c_row))
    pivot = diagonal(gram, 1)
    steps = gram.T / pivot
    low_ref[...] = jnp.where(at_col < at_row, steps, 0.0)
    later = jnp.where(at_col > at_row, steps, 0.0)
    pre_ref[...] = lax.dot_general(
        later, a_ref[...], (((1,), (1,)), ((), ())), precision=EXACT, preferred_element_type=jnp.float32
    )
    scale_ref[...] = jnp.broadcast_to(1.0 / (norm_b_col * norm_c_col * pivot), scale_ref.shape)
    count, tile = shape[0] // TILE, within_ref.shape[1:]
    at = 0
    for column in range(shape[0]):
        own = column // TILE
        for t in range(own, count):
            weights = jnp.broadcast_to(
                low_ref[t * TILE : (t + 1) * TILE, column : column + 1], tile
            )
            if t == own:
                within_ref[column] = weights
            else:
                after_ref[at] = weights
                at += 1


def sweep_kernel(within_ref, after_ref, pre_ref, scale_ref, *refs):
    sums, out_ref = refs[:-1], refs[-1]
    rank, rows = pre_ref.shape
    total = sums[0][...]
    for ref in sums[1:]:
        total += ref[...]
    start = total.T * scale_ref[...] - pre_ref[...]
    count = rank // TILE
    tile = (TILE, rows)
    place = lax.broadcasted_iota(jnp.int32, tile, 0)
    rest = [start[t * TILE : (t + 1) * TILE] for t in range(count)]
    at = 0
    for k in range(count):
        wide = [jnp.broadcast_to(rest[k][s : s + 1], tile) for s in range(TILE)]
        for s in range(TILE):
            done = wide[s] = jnp.maximum(wide[s], 0.0)
            column = k * TILE + s
            for t in range(s + 1, TILE):
                wide[t] = wide[t] - jnp.broadcast_to(within_ref[column, t : t + 1], tile) * done
            for t in range(k + 1, count):
                rest[t] = rest[t] - after_ref[at] * done
                at += 1
        rest[k] = wide[0]
        for s in range(1, TILE):
            rest[k] = jnp.where(place == s, wide[s], rest[k])
    out_ref[...] = jnp.concatenate(rest, 0).T


def body(blocks, coords, factor_a, factor_b, factor_c):
    n_grp = lax.axis_size("grp")
    n_rep = lax.axis_size("rep")
    n_x = n_grp // CORES
    near = 2 if n_rep % 2 == 0 else 1
    line = n_rep // near
    nblk = blocks.shape[0]
    rank = factor_a.shape[1]
    tiles = rank // TILE
    id_rows = -(-nblk // TILE) * TILE
    jb = factor_b.shape[0] // BS
    ab = factor_a.shape[0] // BS
    params = pltpu.CompilerParams(vmem_limit_bytes=16 * 2**20)

    def move(value, chips, swap, beside=0, along=0):
        def to(x, c, rep):
            to_rep = partner(rep // near, along, line) * near + ((rep + beside) % near)
            return (x + chips) % n_x, c ^ swap, to_rep

        return lax.ppermute(value, ("grp", "rep"), moves(n_grp, n_rep, to))

    asks = [move(coords, d, 1) for d in range(1, n_x)]
    mate_b = move(factor_b, 0, 1)
    mate_c = move(factor_c, 0, 1)
    own_b, own_c = pl.pallas_call(
        load_kernel,
        out_shape=[jax.ShapeDtypeStruct(factor_b.shape, factor_b.dtype)] * 2,
        in_specs=[HBM] * 2,
        out_specs=[VMEM] * 2,
        scratch_shapes=[pltpu.SemaphoreType.DMA((2,))],
        compiler_params=params,
        name="load_shards",
    )(
        pltpu.with_memory_space_constraint(factor_b, pltpu.HBM),
        pltpu.with_memory_space_constraint(factor_c, pltpu.HBM),
    )
    factors = (own_b, mate_b, own_c, mate_c)

    chip_gram = pl.pallas_call(
        gram_kernel,
        out_shape=jax.ShapeDtypeStruct((2, rank, rank), jnp.float32),
        in_specs=[VMEM] * 4,
        out_specs=VMEM,
        compiler_params=params,
        name="chip_gram",
    )(*factors)

    answers = pl.pallas_call(
        functools.partial(gather_kernel, n_x - 1, nblk, jb),
        out_shape=[jax.ShapeDtypeStruct((2 * nblk, BS, rank), factor_b.dtype)] * (n_x - 1),
        in_specs=[VMEM] * (n_x - 1) + [VMEM] * 4,
        out_specs=[VMEM] * (n_x - 1),
        compiler_params=params,
        name="gather_rows",
    )(*asks, *factors)
    answers, chip_gram = lax.optimization_barrier((answers, chip_gram))
    found = [move(answers[d - 1], -d, 1) for d in range(1, n_x)]
    grams = [chip_gram] + [move(chip_gram, d, 1) for d in range(1, n_x)]

    local = pl.pallas_call(
        functools.partial(local_kernel, n_x, nblk, jb),
        out_shape=[
            jax.ShapeDtypeStruct((2 * nblk, BS, rank), factor_b.dtype),
            jax.ShapeDtypeStruct((2 * nblk, TILE, rank), jnp.int32),
            jax.ShapeDtypeStruct((id_rows, rank), jnp.float32),
        ],
        in_specs=[VMEM] * 5,
        out_specs=[VMEM] * 3,
        compiler_params=params,
        name="local_rows",
    )(coords, *factors)
    found, local = lax.optimization_barrier((found, local))

    partial = pl.pallas_call(
        functools.partial(partial_kernel, n_x, nblk),
        out_shape=jax.ShapeDtypeStruct((nblk * BS + id_rows, rank), jnp.float32),
        in_specs=[VMEM] * (3 + n_x),
        out_specs=VMEM,
        compiler_params=params,
        name="block_products",
    )(*local, *found, blocks)
    offsets = [(d, b) for d in range(n_x) for b in range(near) if d or b]

    def spread(value, pair):
        def to(x, c, rep):
            chips, beside = pair[(x + c + rep % near) % 2]
            to_rep = rep // near * near + (rep + beside) % near
            return (x + chips) % n_x, (c + chips + beside) % CORES, to_rep

        return lax.ppermute(value, ("grp", "rep"), moves(n_grp, n_rep, to))

    others = [spread(partial, pair) for pair in zip(offsets, reversed(offsets))]
    prepared = pl.pallas_call(
        functools.partial(prepare_kernel, n_x),
        out_shape=[
            jax.ShapeDtypeStruct((rank, TILE, ab * BS), jnp.float32),
            jax.ShapeDtypeStruct((tiles * (tiles - 1) // 2 * TILE, TILE, ab * BS), jnp.float32),
            jax.ShapeDtypeStruct((rank, ab * BS), jnp.float32),
            jax.ShapeDtypeStruct((rank, ab * BS), jnp.float32),
        ],
        in_specs=[VMEM] * (n_x + 1),
        out_specs=[VMEM] * 4,
        scratch_shapes=[pltpu.VMEM((rank, rank), jnp.float32)],
        compiler_params=params,
        name="prepare_sweep",
    )(*grams, factor_a)
    arrived = [partial, move(partial, 0, 1), *others, *(move(value, 0, 1) for value in others)]

    def sums_for(places, inputs, name):
        return pl.pallas_call(
            functools.partial(owner_kernel, places, nblk, n_rep, near, ab, len(inputs)),
            out_shape=[jax.ShapeDtypeStruct(factor_a.shape, jnp.float32)] * len(places),
            in_specs=[VMEM] * len(inputs),
            out_specs=[VMEM] * len(places),
            compiler_params=params,
            name=name,
        )(*inputs)

    order = range(line - 1, 0, -1)
    leaving = sums_for(order, arrived, "sums_to_send")
    arrived, leaving = lax.optimization_barrier((arrived, leaving))
    staying = sums_for((0,), arrived, "own_sum")
    sums = [*staying] + [move(value, 0, 1, 0, d) for d, value in zip(order, leaving)]

    return pl.pallas_call(
        sweep_kernel,
        out_shape=jax.ShapeDtypeStruct(factor_a.shape, jnp.float32),
        in_specs=[VMEM] * (4 + line),
        out_specs=VMEM,
        compiler_params=params,
        name="sweep",
    )(*prepared, *sums)


def solution(mesh):
    placed = (
        P(("grp", "rep"), None, None),
        P(("grp", "rep"), None),
        P(("grp", "rep"), None),
        P("grp", None),
        P("grp", None),
    )
    return jax.shard_map(
        body, mesh=mesh, in_specs=placed, out_specs=P(("grp", "rep"), None), check_vma=False
    )
```

```python
import functools

import jax
import jax.numpy as jnp
from jax import lax
from jax.experimental import pallas as pl
from jax.experimental.pallas import tpu as pltpu
from jax.sharding import PartitionSpec as P

BS = 64
TILE = 8
CORES = 2
EXACT = lax.Precision.HIGHEST
VMEM = pl.BlockSpec(memory_space=pltpu.VMEM)
HBM = pl.BlockSpec(memory_space=pltpu.HBM)


def moves(n_grp, n_rep, to):
    pairs = []
    for g in range(n_grp):
        for rep in range(n_rep):
            x, c, to_rep = to(g // CORES, g % CORES, rep)
            pairs.append((g * n_rep + rep, (x * CORES + c) * n_rep + to_rep))
    return pairs


def partner(index, offset, size):
    return index ^ offset if size & (size - 1) == 0 else (index + offset) % size


def here():
    grp = lax.axis_index("grp")
    return lax.div(grp, CORES), lax.rem(grp, CORES), lax.axis_index("rep")


def load_kernel(b_ref, c_ref, own_b, own_c, sems):
    copies = [
        pltpu.make_async_copy(src, dst, sems.at[i])
        for i, (src, dst) in enumerate(((b_ref, own_b), (c_ref, own_c)))
    ]
    for copy in copies:
        copy.start()
    for copy in copies:
        copy.wait()


def gram_kernel(own_b, mate_b, own_c, mate_c, out_ref):
    dims = (((0,), (0,)), ((), ()))
    for mode, shards in enumerate(((own_b, mate_b), (own_c, mate_c))):
        total = 0.0
        for ref in shards:
            total += lax.dot_general(ref[...], ref[...], dims, preferred_element_type=jnp.float32)
        out_ref[mode] = total


def row_block(own, mate, local, core, jb):
    row = pl.multiple_of(lax.rem(local, jb) * BS, BS)
    return jnp.where(lax.div(local, jb) == core, own[pl.ds(row, BS)], mate[pl.ds(row, BS)])


def gather_kernel(n_ask, nblk, jb, *refs):
    asks, factors, outs = refs[:n_ask], refs[n_ask : n_ask + 4], refs[n_ask + 4 :]
    _, core, _ = here()
    for ask, out in zip(asks, outs):
        for mode in range(2):
            for n in range(nblk):
                local = lax.rem(ask[...][n, 1 + mode], CORES * jb)
                out[mode * nblk + n] = row_block(*factors[2 * mode : 2 * mode + 2], local, core, jb)


def local_kernel(n_x, nblk, jb, ask_ref, *refs):
    factors, (rows_ref, far_ref, first_ref) = refs[:4], refs[4:]
    ask = ask_ref[...]
    my_x, core, _ = here()
    for mode in range(2):
        for n in range(nblk):
            slot = mode * nblk + n
            wanted = ask[n, 1 + mode]
            local = lax.rem(wanted, CORES * jb)
            rows_ref[slot] = row_block(*factors[2 * mode : 2 * mode + 2], local, core, jb)
            far = lax.rem(lax.div(wanted, CORES * jb) - my_x + n_x, n_x)
            far_ref[slot] = jnp.full(far_ref.shape[1:], far, jnp.int32)
    place = lax.broadcasted_iota(jnp.int32, first_ref.shape, 0)
    first = jnp.zeros(first_ref.shape, jnp.int32)
    for n in range(nblk):
        first = jnp.where(place == n, ask[n, 0], first)
    first_ref[...] = first.astype(jnp.float32)


def partial_kernel(n_x, nblk, rows_ref, far_ref, first_ref, *refs):
    found, blocks_ref, out_ref = refs[:-2], refs[-2], refs[-1]

    def rows_of(n, mode):
        slot = mode * nblk + n
        rows = rows_ref[slot]
        for d in range(1, n_x):
            rows = jnp.where(far_ref[slot, :1] == d, found[d - 1][slot], rows)
        return rows

    step = 16
    for n in range(nblk):
        left, right = rows_of(n, 0), rows_of(n, 1)
        rank = left.shape[1]
        total = jnp.zeros((BS, rank), jnp.float32)
        for j in range(0, BS, step):
            khatri = left[j : j + step, None, :] * right[None, :, :]
            total += jnp.dot(
                blocks_ref[n, :, j * BS : (j + step) * BS],
                khatri.reshape(step * BS, rank),
                preferred_element_type=jnp.float32,
            )
        out_ref[n * BS : (n + 1) * BS] = total
    out_ref[nblk * BS :] = first_ref[...]


def owner_kernel(places, nblk, n_rep, near, ab, count, *refs):
    arrived, outs = refs[:count], refs[count:]
    my_x, core, rep = here()
    line = n_rep // near
    at, side = lax.div(rep, near), lax.rem(rep, near)
    for offset, out in zip(places, outs):
        if line & (line - 1) == 0:
            to_at = lax.bitwise_xor(at, offset)
        else:
            to_at = lax.rem(at + offset, line)
        to_core = core if offset == 0 else 1 - core
        first = ((my_x * CORES + to_core) * n_rep + to_at * near + side) * ab
        for sub in range(ab):
            target = (first + sub).astype(jnp.float32)
            total = None
            for ref in arrived:
                for n in range(nblk):
                    at_id = nblk * BS + n
                    term = jnp.where(
                        ref[at_id : at_id + 1] == target, ref[n * BS : (n + 1) * BS], 0.0
                    )
                    total = term if total is None else total + term
            out[sub * BS : (sub + 1) * BS] = total


def prepare_kernel(n_x, *refs):
    grams = refs[:n_x]
    a_ref, within_ref, after_ref, pre_ref, scale_ref, low_ref = refs[n_x:]
    gram_b, gram_c = grams[0][0], grams[0][1]
    for ref in grams[1:]:
        gram_b += ref[0]
        gram_c += ref[1]
    shape = gram_b.shape
    at_row = lax.broadcasted_iota(jnp.int32, shape, 0)
    at_col = lax.broadcasted_iota(jnp.int32, shape, 1)

    def diagonal(square, axis):
        return jnp.sum(jnp.where(at_row == at_col, square, 0.0), axis=axis, keepdims=True)

    norm_b_row, norm_b_col = jnp.sqrt(diagonal(gram_b, 0)), jnp.sqrt(diagonal(gram_b, 1))
    norm_c_row, norm_c_col = jnp.sqrt(diagonal(gram_c, 0)), jnp.sqrt(diagonal(gram_c, 1))
    gram = gram_b / (norm_b_col * norm_b_row) * (gram_c / (norm_c_col * norm_c_row))
    pivot = diagonal(gram, 1)
    steps = gram.T / pivot
    low_ref[...] = jnp.where(at_col < at_row, steps, 0.0)
    later = jnp.where(at_col > at_row, steps, 0.0)
    pre_ref[...] = lax.dot_general(
        later, a_ref[...], (((1,), (1,)), ((), ())), precision=EXACT, preferred_element_type=jnp.float32
    )
    scale_ref[...] = jnp.broadcast_to(1.0 / (norm_b_col * norm_c_col * pivot), scale_ref.shape)
    count, tile = shape[0] // TILE, within_ref.shape[1:]
    at = 0
    for column in range(shape[0]):
        own = column // TILE
        for t in range(own, count):
            weights = jnp.broadcast_to(
                low_ref[t * TILE : (t + 1) * TILE, column : column + 1], tile
            )
            if t == own:
                within_ref[column] = weights
            else:
                after_ref[at] = weights
                at += 1


def sweep_kernel(within_ref, after_ref, pre_ref, scale_ref, *refs):
    sums, out_ref = refs[:-1], refs[-1]
    rank, rows = pre_ref.shape
    total = sums[0][...]
    for ref in sums[1:]:
        total += ref[...]
    start = total.T * scale_ref[...] - pre_ref[...]
    count = rank // TILE
    tile = (TILE, rows)
    place = lax.broadcasted_iota(jnp.int32, tile, 0)
    rest = [start[t * TILE : (t + 1) * TILE] for t in range(count)]
    at = 0
    for k in range(count):
        wide = [jnp.broadcast_to(rest[k][s : s + 1], tile) for s in range(TILE)]
        for s in range(TILE):
            done = wide[s] = jnp.maximum(wide[s], 0.0)
            column = k * TILE + s
            for t in range(s + 1, TILE):
                wide[t] = wide[t] - jnp.broadcast_to(within_ref[column, t : t + 1], tile) * done
            for t in range(k + 1, count):
                rest[t] = rest[t] - after_ref[at] * done
                at += 1
        rest[k] = wide[0]
        for s in range(1, TILE):
            rest[k] = jnp.where(place == s, wide[s], rest[k])
    out_ref[...] = jnp.concatenate(rest, 0).T


def body(blocks, coords, factor_a, factor_b, factor_c):
    n_grp = lax.axis_size("grp")
    n_rep = lax.axis_size("rep")
    n_x = n_grp // CORES
    near = 2 if n_rep % 2 == 0 else 1
    line = n_rep // near
    nblk = blocks.shape[0]
    rank = factor_a.shape[1]
    tiles = rank // TILE
    id_rows = -(-nblk // TILE) * TILE
    jb = factor_b.shape[0] // BS
    ab = factor_a.shape[0] // BS
    params = pltpu.CompilerParams(vmem_limit_bytes=16 * 2**20)

    def move(value, chips, swap, beside=0, along=0):
        def to(x, c, rep):
            to_rep = partner(rep // near, along, line) * near + ((rep + beside) % near)
            return (x + chips) % n_x, c ^ swap, to_rep

        return lax.ppermute(value, ("grp", "rep"), moves(n_grp, n_rep, to))

    asks = [move(coords, d, 1) for d in range(1, n_x)]
    mate_b = move(factor_b, 0, 1)
    mate_c = move(factor_c, 0, 1)
    own_b, own_c = pl.pallas_call(
        load_kernel,
        out_shape=[jax.ShapeDtypeStruct(factor_b.shape, factor_b.dtype)] * 2,
        in_specs=[HBM] * 2,
        out_specs=[VMEM] * 2,
        scratch_shapes=[pltpu.SemaphoreType.DMA((2,))],
        compiler_params=params,
        name="load_shards",
    )(
        pltpu.with_memory_space_constraint(factor_b, pltpu.HBM),
        pltpu.with_memory_space_constraint(factor_c, pltpu.HBM),
    )
    factors = (own_b, mate_b, own_c, mate_c)

    chip_gram = pl.pallas_call(
        gram_kernel,
        out_shape=jax.ShapeDtypeStruct((2, rank, rank), jnp.float32),
        in_specs=[VMEM] * 4,
        out_specs=VMEM,
        compiler_params=params,
        name="chip_gram",
    )(*factors)

    answers = pl.pallas_call(
        functools.partial(gather_kernel, n_x - 1, nblk, jb),
        out_shape=[jax.ShapeDtypeStruct((2 * nblk, BS, rank), factor_b.dtype)] * (n_x - 1),
        in_specs=[VMEM] * (n_x - 1) + [VMEM] * 4,
        out_specs=[VMEM] * (n_x - 1),
        compiler_params=params,
        name="gather_rows",
    )(*asks, *factors)
    answers, chip_gram = lax.optimization_barrier((answers, chip_gram))
    found = [move(answers[d - 1], -d, 1) for d in range(1, n_x)]
    grams = [chip_gram] + [move(chip_gram, d, 1) for d in range(1, n_x)]

    local = pl.pallas_call(
        functools.partial(local_kernel, n_x, nblk, jb),
        out_shape=[
            jax.ShapeDtypeStruct((2 * nblk, BS, rank), factor_b.dtype),
            jax.ShapeDtypeStruct((2 * nblk, TILE, rank), jnp.int32),
            jax.ShapeDtypeStruct((id_rows, rank), jnp.float32),
        ],
        in_specs=[VMEM] * 5,
        out_specs=[VMEM] * 3,
        compiler_params=params,
        name="local_rows",
    )(coords, *factors)
    found, local = lax.optimization_barrier((found, local))

    partial = pl.pallas_call(
        functools.partial(partial_kernel, n_x, nblk),
        out_shape=jax.ShapeDtypeStruct((nblk * BS + id_rows, rank), jnp.float32),
        in_specs=[VMEM] * (3 + n_x),
        out_specs=VMEM,
        compiler_params=params,
        name="block_products",
    )(*local, *found, blocks)
    offsets = [(d, b) for d in range(n_x) for b in range(near) if d or b]

    def spread(value, pair):
        def to(x, c, rep):
            chips, beside = pair[(x + c + rep % near) % 2]
            to_rep = rep // near * near + (rep + beside) % near
            return (x + chips) % n_x, (c + chips + beside) % CORES, to_rep

        return lax.ppermute(value, ("grp", "rep"), moves(n_grp, n_rep, to))

    others = [spread(partial, pair) for pair in zip(offsets, reversed(offsets))]
    prepared = pl.pallas_call(
        functools.partial(prepare_kernel, n_x),
        out_shape=[
            jax.ShapeDtypeStruct((rank, TILE, ab * BS), jnp.float32),
            jax.ShapeDtypeStruct((tiles * (tiles - 1) // 2 * TILE, TILE, ab * BS), jnp.float32),
            jax.ShapeDtypeStruct((rank, ab * BS), jnp.float32),
            jax.ShapeDtypeStruct((rank, ab * BS), jnp.float32),
        ],
        in_specs=[VMEM] * (n_x + 1),
        out_specs=[VMEM] * 4,
        scratch_shapes=[pltpu.VMEM((rank, rank), jnp.float32)],
        compiler_params=params,
        name="prepare_sweep",
    )(*grams, factor_a)
    arrived = [partial, move(partial, 0, 1), *others, *(move(value, 0, 1) for value in others)]

    def sums_for(places, inputs, name):
        return pl.pallas_call(
            functools.partial(owner_kernel, places, nblk, n_rep, near, ab, len(inputs)),
            out_shape=[jax.ShapeDtypeStruct(factor_a.shape, jnp.float32)] * len(places),
            in_specs=[VMEM] * len(inputs),
            out_specs=[VMEM] * len(places),
            compiler_params=params,
            name=name,
        )(*inputs)

    order = range(line - 1, 0, -1)
    leaving = sums_for(order, arrived, "sums_to_send")
    arrived, leaving = lax.optimization_barrier((arrived, leaving))
    staying = sums_for((0,), arrived, "own_sum")
    sums = [*staying] + [move(value, 0, 1, 0, d) for d, value in zip(order, leaving)]

    return pl.pallas_call(
        sweep_kernel,
        out_shape=jax.ShapeDtypeStruct(factor_a.shape, jnp.float32),
        in_specs=[VMEM] * (4 + line),
        out_specs=VMEM,
        compiler_params=params,
        name="sweep",
    )(*prepared, *sums)


def solution(mesh):
    placed = (
        P(("grp", "rep"), None, None),
        P(("grp", "rep"), None),
        P(("grp", "rep"), None),
        P("grp", None),
        P("grp", None),
    )
    return jax.shard_map(
        body, mesh=mesh, in_specs=placed, out_specs=P(("grp", "rep"), None), check_vma=False
    )
```
